32 devices in a mesh: group: 4 (over y, x), leaf: 8 (over z, core).
Axes of the slice: x: 2, y: 2, z: 4, core: 2. Of those that a mesh axis runs over, the one named last changes fastest.
Arguments:
- right_sides: float32 [16, 131072], P(None, ('group', 'leaf')), may hold values from -6 to 6
- near_blocks: float32 [2048, 8, 4096], P(('group', 'leaf')), may hold values from -0.375 to 0.375
- near_source: int32 [2048, 8], P(('group', 'leaf')), may hold values from 0 to 2047, as said below
- near_count: int32 [2048], P(('group', 'leaf')), may hold values from 1 to 8
- basis: float32 [2048, 2048], P(('group', 'leaf')), may hold values from -0.75 to 0.75
- leaf_source: int32 [2048, 8], P(('group', 'leaf')), may hold values from 0 to 2047
- leaf_coupling: float32 [2048, 8, 1024], P(('group', 'leaf')), may hold values from -0.375 to 0.375
- leaf_transfer: float32 [2048, 1024], P(('group', 'leaf')), may hold values from -1 to 1
- cluster_source: int32 [128, 8], P(('group', 'leaf')), may hold values from 0 to 31
- cluster_coupling: float32 [128, 8, 1024], P(('group', 'leaf')), may hold values from -0.09375 to 0.09375
- cluster_transfer: float32 [128, 1024], P(('group', 'leaf')), may hold values from -1 to 1
- group_coupling: float32 [4, 4, 1024], P('group'), may hold values from -0.0234375 to 0.0234375
Outputs:
- applied: float32 [16, 131072], P(None, ('group', 'leaf'))
The draws below stay inside these ranges and needn't reach their ends.
Inputs may be any that keep to these rules, and one draw needn't show every extreme that they name: near_source[t, j] and leaf_source[t, j] name a leaf held by the same device as t or by the device just before or after it in the order of devices.
All inputs are finite; a program needn't handle non-finite values.
Results may differ from the reference program's by a relative error of at most 0.0001.
Values sent between devices are 32-bit elements; how exact they have to be, the bound alone decides.
A program may use at most 128 MiB of HBM per device.

```python
import jax
import jax.numpy as jnp
from jax import lax

LEAF = 64
K = 32
RHS = 16
LPD = 64
CPD = 4
NEAR = 8
FAR0 = 8
FAR1 = 8
DEVS = 32
GROUPS = 4
LEAVES = 2048
POINTS = 131072
CLUSTERS_ALL = 128
GROUP_CLUSTERS = 32


def window_sources(key, slots):
    leaf_ids = jnp.arange(LEAVES, dtype=jnp.int32)
    first_leaf = leaf_ids // LPD * LPD
    offsets = jax.random.randint(key, (LEAVES, slots), -LPD, 2 * LPD)
    chosen = jnp.clip(first_leaf[:, None] + offsets, 0, LEAVES - 1)
    chosen = chosen.at[0, 0].set(0)
    chosen = chosen.at[LEAVES - 1, slots - 1].set(LEAVES - 1)
    return chosen.astype(jnp.int32)


def draw_near_source(key, part):
    return window_sources(jax.random.fold_in(key, 11), NEAR)


def draw_leaf_source(key, part):
    return window_sources(jax.random.fold_in(key, 12), FAR0)


def draw_near_count(key, part):
    first_key = jax.random.fold_in(key, 21)
    second_key = jax.random.fold_in(key, 22)
    ceilings = jax.random.randint(first_key, (DEVS,), 1, NEAR + 1).at[0].set(NEAR)
    per_leaf = jnp.repeat(ceilings, LPD)
    raw_values = jax.random.randint(second_key, (LEAVES,), 0, 1048576)
    counts = raw_values % per_leaf + 1
    counts = counts.at[0].set(NEAR)
    return counts.astype(jnp.int32)


def plant(entries, rng, least, high):
    shape = entries.shape
    place = [jax.random.randint(jax.random.fold_in(rng, axis), (), 0, shape[axis]) for axis in range(len(shape))]
    entries = entries.at[tuple(place)].set(least)
    longest = shape.index(max(shape))
    place[longest] = (place[longest] + 1) % shape[longest]
    return entries.at[tuple(place)].set(high)


def levels(key, shape, pieces, low, top_value):
    factor_of, own = 1.0, jax.random.fold_in(key, 6)
    for position, blocks in pieces:
        steps = jnp.exp(jax.random.uniform(jax.random.fold_in(own, position), (blocks,), jnp.float32, low / len(pieces), top_value / len(pieces)))
        factor_of = factor_of * jnp.repeat(steps, shape[position] // blocks).reshape([-1 if axis == position else 1 for axis in range(len(shape))])
    return factor_of


def centred(stream_key, dims, deviation, reach, split=(), held_as=jnp.bfloat16):
    result = jax.random.normal(stream_key, dims, jnp.float32) * deviation
    if len(split) > 0:
        result = levels(stream_key, dims, split, -0.22, 0.18) * result
    return jnp.clip(result, min=-reach, max=reach).astype(held_as)


def setup_inputs(seed: int = 0) -> dict:
    key_of = jax.random.split(jax.random.key(seed), 13)
    right_sides = centred(key_of[0], (RHS, POINTS), 1.0, 6.0, ((1, 32),), jnp.float32)
    near_blocks = centred(key_of[1], (LEAVES, NEAR, LEAF * LEAF), (LEAF * NEAR // 2) ** -0.5, 0.375, ((0, 32),), jnp.float32)
    near_source = draw_near_source(jax.random.fold_in(key_of[12], 71), 0)
    near_count = draw_near_count(jax.random.fold_in(key_of[12], 71), 0)
    basis = centred(key_of[4], (LEAVES, K * LEAF), LEAF ** -0.5, 0.75, ((0, 32),), jnp.float32)
    leaf_source = draw_leaf_source(jax.random.fold_in(key_of[12], 71), 0)
    leaf_coupling = centred(key_of[6], (LEAVES, FAR0, K * K), (K * FAR0) ** -0.5, 0.375, ((0, 32),), jnp.float32)
    leaf_transfer = centred(key_of[7], (LEAVES, K * K), K ** -0.5, 1.0, ((0, 32),), jnp.float32)
    cluster_source = plant(jax.random.randint(key_of[8], (CLUSTERS_ALL, FAR1), 0, GROUP_CLUSTERS), jax.random.fold_in(key_of[8], 1), 0, GROUP_CLUSTERS - 1).astype(jnp.int32)
    cluster_coupling = centred(key_of[9], (CLUSTERS_ALL, FAR1, K * K), (K * FAR1 * LPD // CPD) ** -0.5, 0.09375, ((0, 32),), jnp.float32)
    cluster_transfer = centred(key_of[10], (CLUSTERS_ALL, K * K), K ** -0.5, 1.0, ((0, 32),), jnp.float32)
    group_coupling = centred(key_of[11], (GROUPS, GROUPS, K * K), (K * GROUPS * LPD * GROUP_CLUSTERS // CPD) ** -0.5, 0.0234375, ((0, 4),), jnp.float32)
    return {"right_sides": right_sides, "near_blocks": near_blocks, "near_source": near_source, "near_count": near_count, "basis": basis, "leaf_source": leaf_source, "leaf_coupling": leaf_coupling, "leaf_transfer": leaf_transfer, "cluster_source": cluster_source, "cluster_coupling": cluster_coupling, "cluster_transfer": cluster_transfer, "group_coupling": group_coupling}


highest_precision = lax.Precision.HIGHEST


def reference(right_sides, near_blocks, near_source, near_count, basis, leaf_source, leaf_coupling, leaf_transfer, cluster_source, cluster_coupling, cluster_transfer, group_coupling):
    blocks = right_sides.reshape(RHS, LEAVES, LEAF).transpose(1, 0, 2)
    bases = basis.reshape(LEAVES, K, LEAF)
    leaf_coef = jnp.einsum('tka,tra->tkr', bases, blocks, precision=highest_precision)

    def near_step(slot_index, running):
        picked = jnp.take(blocks, near_source[:, slot_index], axis=0)
        slab = lax.dynamic_index_in_dim(near_blocks, slot_index, axis=1, keepdims=False).reshape(LEAVES, LEAF, LEAF)
        live = (near_count > slot_index).astype(jnp.float32)
        term = jnp.einsum('tab,trb->tra', slab, picked, precision=highest_precision)
        return running + term * live[:, None, None]

    near_total = lax.fori_loop(0, NEAR, near_step, jnp.zeros((LEAVES, RHS, LEAF), jnp.float32))

    picked_coef = jnp.take(leaf_coef, leaf_source, axis=0)
    leaf_far = jnp.einsum('tjkl,tjlr->tkr', leaf_coupling.reshape(LEAVES, FAR0, K, K), picked_coef, precision=highest_precision)

    transfers = leaf_transfer.reshape(LEAVES, K, K)
    lifted = jnp.einsum('tkl,tlr->tkr', transfers, leaf_coef, precision=highest_precision)
    cluster_coef = lifted.reshape(CLUSTERS_ALL, LPD // CPD, K, RHS).sum(axis=1)
    upper = cluster_transfer.reshape(CLUSTERS_ALL, K, K)
    projected = jnp.einsum('ukl,ulr->ukr', upper, cluster_coef, precision=highest_precision)
    group_coef = projected.reshape(GROUPS, GROUP_CLUSTERS, K, RHS).sum(axis=1)
    group_field = jnp.einsum('ghkl,hlr->gkr', group_coupling.reshape(GROUPS, GROUPS, K, K), group_coef, precision=highest_precision)

    owners = (jnp.arange(CLUSTERS_ALL, dtype=jnp.int32) // GROUP_CLUSTERS) * GROUP_CLUSTERS
    global_source = owners[:, None] + cluster_source
    picked_cluster = jnp.take(cluster_coef, global_source, axis=0)
    cluster_far = jnp.einsum('ujkl,ujlr->ukr', cluster_coupling.reshape(CLUSTERS_ALL, FAR1, K, K), picked_cluster, precision=highest_precision)
    spread_top = jnp.repeat(group_field, GROUP_CLUSTERS, axis=0)
    cluster_field = cluster_far + jnp.einsum('ulk,ulr->ukr', upper, spread_top, precision=highest_precision)
    spread_cluster = jnp.repeat(cluster_field, LPD // CPD, axis=0)
    leaf_field = leaf_far + jnp.einsum('tlk,tlr->tkr', transfers, spread_cluster, precision=highest_precision)
    total = near_total + jnp.einsum('tka,tkr->tra', bases, leaf_field, precision=highest_precision)
    return total.transpose(1, 0, 2).reshape(RHS, POINTS)
```

```python
import functools

import jax
import jax.numpy as jnp
from jax import lax
from jax.experimental import pallas as pl
from jax.experimental.pallas import tpu as pltpu
from jax.sharding import PartitionSpec as P

LEAF = 64
K = 32
RHS = 16
FAR0 = 8
FAR1 = 8
NEAR = 8
LANES = 128
KR = K * RHS
KK = K * K
CHUNK = 8

f32 = jnp.float32
bf16 = jnp.bfloat16
MESH = pl.DeviceIdType.MESH
VMEM = pl.BlockSpec(memory_space=pltpu.VMEM)
SMEM = pl.BlockSpec(memory_space=pltpu.SMEM)
NT = (((1,), (1,)), ((), ()))
NN = (((1,), (0,)), ((), ()))


def halves(value):
    high = value.astype(bf16)
    low = (value - high.astype(f32)).astype(bf16)
    return high, low


def mm(a, b, dims=NN):
    return lax.dot_general(a, b, dims, preferred_element_type=f32)


def pick(value, chosen):
    high, low = halves(value)
    return mm(high, chosen) + mm(low, chosen)


def iota(shape, dim):
    return lax.broadcasted_iota(jnp.int32, shape, dim)


def mask(condition):
    return jnp.where(condition, 1.0, 0.0).astype(bf16)


def doubled_pair(pair):
    first = iota(pair.shape, 1) < LEAF
    turned = pltpu.roll(pair, LEAF, 1)
    zero = jnp.zeros_like(pair)
    even = jnp.concatenate([jnp.where(first, pair, zero), jnp.where(first, zero, turned)], axis=0)
    odd = jnp.concatenate([jnp.where(first, turned, zero), jnp.where(first, zero, pair)], axis=0)
    return even, odd


def coef_kernel(x_ref, basis_ref, coef_ref):
    def step(p, carry):
        pair = x_ref[:, pl.ds(pl.multiple_of(p * LANES, LANES), LANES)]
        for side, doubled in enumerate(doubled_pair(pair)):
            xh, xl = halves(doubled)
            bh, bl = halves(basis_ref[2 * p + side])
            both = jnp.concatenate([bh, bl], axis=1)
            twice = jnp.concatenate([xh, xh], axis=1)
            coef_ref[2 * p + side] = mm(both, twice, NT) + mm(bh, xl, NT)
        return carry

    lax.fori_loop(0, basis_ref.shape[0] // 2, step, 0, unroll=4)


def turn(src, rows, dst_ref, lane):
    here = min(LANES, src.shape[0] - rows)
    for c in range(src.shape[1] // LANES):
        block = src[rows : rows + here, c * LANES : (c + 1) * LANES]
        if here < LANES:
            block = jnp.concatenate([block, jnp.zeros((LANES - here, LANES), f32)], axis=0)
        dst_ref[c * LANES : (c + 1) * LANES, lane : lane + LANES] = block.T


def small_products(at_ref, g_ref, out_ref, tiles, transposed=False):
    width = 8

    def step(i, carry):
        tile, kb = i // (K // width), i % (K // width)
        lanes = pl.ds(pl.multiple_of(tile * LANES, LANES), LANES)
        acc = [jnp.zeros((RHS, LANES), f32)] * width
        for l8 in range(0, K, 8):
            if transposed:
                at = [at_ref[pl.ds(pl.multiple_of(kb * 8, 8) + l * K, 8), lanes] for l in range(l8, l8 + 8)]
            else:
                at = [at_ref[pl.ds(pl.multiple_of(kb * 8 * K, 8 * K) + j * K + l8, 8), lanes] for j in range(width)]
            for i in range(8):
                g = g_ref[(l8 + i) * RHS : (l8 + i + 1) * RHS, lanes]
                for j in range(width):
                    row = at[i][j : j + 1] if transposed else at[j][i : i + 1]
                    acc[j] = acc[j] + row * g
        for j in range(width):
            start = pl.multiple_of(kb * (width * RHS) + j * RHS, RHS)
            out_ref[pl.ds(start, RHS), lanes] = acc[j]
        return carry

    lax.fori_loop(0, tiles * (K // width), step, 0)


def up_kernel(base, cpd, coef_ref, transfer_ref, small_ref, out_ref, et, ct, st, work):
    leaves = coef_ref.shape[0]
    per = leaves // cpd
    turn(coef_ref, 0, ct, 0)
    turn(transfer_ref, 0, et, 0)
    turn(small_ref, 0, st, 0)
    small_products(et, ct, work, 1)
    t, q = iota((LANES, LANES), 0), iota((LANES, LANES), 1)
    chosen = mask((q - base == t // per) & (t < leaves))
    ct[...] = pick(work[...], chosen)
    small_products(st, ct, work, 1)
    for c in range(KR // LANES):
        rows = slice(c * LANES, (c + 1) * LANES)
        out_ref[0:8, rows] = ct[rows, :].T[base : base + 8]
        total = jnp.sum(work[rows, :].T[base : base + cpd], axis=0, keepdims=True)
        out_ref[8:16, rows] = jnp.broadcast_to(total, (8, LANES))


def down_kernel(base, cpd, groups, coef_ref, near_coef_ref, transfer_ref, coupling_ref, small_ref, cluster_ref, group_ref,
                leaf_idx_ref, cluster_idx_ref, field_ref, et, ct, st, lt, gt, gl, work, lwork, small_g):
    leaves = transfer_ref.shape[0]
    per = leaves // cpd
    slots = leaves * FAR0
    turn(transfer_ref, 0, et, 0)
    turn(small_ref, 0, st, 0)
    for tile in range(slots // LANES):
        turn(coupling_ref, tile * LANES, lt, tile * LANES)
    for part in range(-(-coef_ref.shape[0] // LANES)):
        turn(coef_ref, part * LANES, ct, part * LANES)
    sources = ct.shape[1]
    onehot = mask(iota((sources, slots), 0) == leaf_idx_ref[...])
    gl[...] = pick(ct[...], onehot)
    small_products(lt, gl, lwork, slots // LANES)
    rows = cluster_ref.shape[0]
    count = gt.shape[1]
    for part in range(count // LANES):
        if part * LANES < rows:
            turn(cluster_ref, part * LANES, gt, part * LANES)
        else:
            turn(group_ref, 0, gt, part * LANES)
    onehot = mask(iota((count, LANES), 0) == cluster_idx_ref[...])
    small_g[...] = pick(gt[...], onehot)
    small_products(st, small_g, work, 1)
    a, b = iota((LANES, LANES), 0), iota((LANES, LANES), 1)
    wide = cpd * FAR1
    mine = (b >= base) & (b < base + cpd)
    top = mask((a >= wide) & (a < wide + groups) & mine)
    small_g[...] = pick(work[...], top)
    slot = mask((a < wide) & (b - base == a // FAR1))
    far = pick(work[...], slot)
    small_products(st, small_g, work, 1, transposed=True)
    spread = mask((a - base == b // per) & (b < leaves))
    small_g[...] = pick(far + work[...], spread)
    small_products(et, small_g, work, 1, transposed=True)
    gather = mask(iota((slots, LANES), 0) // FAR0 == iota((slots, LANES), 1))
    field = work[...] + pick(lwork[...], gather)
    for c in range(KR // LANES):
        rows_c = slice(c * LANES, (c + 1) * LANES)
        field_ref[:, rows_c] = field[rows_c].T[:leaves]


def near_kernel(idx_ref, near_ref, before_ref, own_ref, after_ref, basis_ref, field_ref, out_ref, xh_ref, xl_ref, place_ref, part_ref):
    chunk = pl.program_id(0)
    leaves = own_ref.shape[1] // LEAF

    @pl.when(chunk == 0)
    def _():
        for part, ref in enumerate((before_ref, own_ref, after_ref)):

            def build(p, carry, ref=ref, part=part):
                pair = ref[:, pl.ds(pl.multiple_of(p * LANES, LANES), LANES)]
                for side, doubled in enumerate(doubled_pair(pair)):
                    high, low = halves(doubled)
                    xh_ref[part * leaves + 2 * p + side] = high
                    xl_ref[part * leaves + 2 * p + side] = low
                return carry

            lax.fori_loop(0, leaves // 2, build, 0, unroll=4)
        xh_ref[3 * leaves] = jnp.zeros(xh_ref.shape[1:], bf16)
        xl_ref[3 * leaves] = jnp.zeros(xl_ref.shape[1:], bf16)
        row, col = iota((2 * LANES, LANES), 0), iota((2 * LANES, LANES), 1)
        for side in range(2):
            for half in range(2):
                place_ref[2 * side + half] = mask(col == side * LEAF + 2 * (row // NEAR) + half)

    slot_of_lane = iota((2 * RHS, 2 * LANES), 1) % NEAR
    for i in range(CHUNK):
        n = near_ref[i]
        rows = jnp.concatenate([n[:, c * LANES : (c + 1) * LANES] for c in range(LEAF // 2)], axis=0)
        nh, nl = halves(rows)
        weights = jnp.concatenate([nh, nl], axis=1)
        at = [idx_ref[(chunk * CHUNK + i) * NEAR + j] for j in range(NEAR)]
        xh = jnp.concatenate([xh_ref[s] for s in at], axis=0)
        xl = jnp.concatenate([xl_ref[s] for s in at], axis=0)
        full = mm(jnp.concatenate([xh, xh], axis=1), weights, NT) + mm(
            jnp.concatenate([xl, xl], axis=1), weights, NT
        )
        kept = full[: 2 * RHS]
        for j in range(1, NEAR):
            kept = jnp.where(slot_of_lane == j, full[j * 2 * RHS : (j + 1) * 2 * RHS], kept)
        part_ref[i] = kept

    total = jnp.zeros((CHUNK // 2 * RHS, LANES), f32)
    for side in range(2):
        for half in range(2):
            rows = jnp.concatenate(
                [part_ref[2 * p + side, half * RHS : (half + 1) * RHS] for p in range(CHUNK // 2)], axis=0
            )
            total = total + pick(rows, place_ref[2 * side + half])

    first = iota((RHS, LANES), 1) < LEAF
    for p in range(CHUNK // 2):
        ends = []
        for side in range(2):
            i = 2 * p + side
            fh, fl = halves(field_ref[i])
            bh, bl = halves(basis_ref[i])
            wide = mm(jnp.concatenate([fh, fl], axis=0), jnp.concatenate([bh, bl], axis=1))
            both = wide[: 2 * RHS, :LANES] + wide[: 2 * RHS, LANES:] + wide[2 * RHS :, :LANES]
            ends.append((both[:RHS], both[RHS:]))
        straight = jnp.where(first, ends[0][0], ends[1][1])
        crossed = jnp.where(first, ends[1][0], ends[0][1])
        out_ref[:, p * LANES : (p + 1) * LANES] = (
            total[p * RHS : (p + 1) * RHS] + straight + pltpu.roll(crossed, LEAF, 1)
        )


def exchange_kernel(nleaf, ngroup, block_ref, gathered_ref, group_ref, sums, leaf_send, leaf_recv, group_send, group_recv):
    g, z = lax.axis_index("group"), lax.axis_index("leaf")
    barrier = pltpu.get_barrier_semaphore()

    def greet_leaf(d, carry):
        pl.semaphore_signal(barrier, inc=1, device_id=(g, lax.rem(z + d, nleaf)), device_id_type=MESH)
        return carry

    def greet_group(d, carry):
        pl.semaphore_signal(barrier, inc=1, device_id=(lax.rem(g + d, ngroup), z), device_id_type=MESH)
        return carry

    lax.fori_loop(1, nleaf, greet_leaf, 0)
    lax.fori_loop(1, ngroup, greet_group, 0)
    pl.semaphore_wait(barrier, nleaf + ngroup - 2)

    def to_leaf(d):
        peer = lax.rem(z + d, nleaf)
        return pltpu.make_async_remote_copy(
            src_ref=block_ref, dst_ref=gathered_ref.at[z], send_sem=leaf_send.at[d], recv_sem=leaf_recv.at[z],
            device_id=(g, peer), device_id_type=MESH)

    def from_leaf(d):
        peer = lax.rem(z + d, nleaf)
        return pltpu.make_async_remote_copy(
            src_ref=block_ref, dst_ref=gathered_ref.at[peer], send_sem=leaf_send.at[d], recv_sem=leaf_recv.at[peer],
            device_id=(g, peer), device_id_type=MESH)

    def start_leaf(d, carry):
        to_leaf(d).start()
        return carry

    lax.fori_loop(1, nleaf, start_leaf, 0)
    gathered_ref[z] = block_ref[...]

    def wait_leaf(d, carry):
        from_leaf(d).wait()
        return carry

    lax.fori_loop(1, nleaf, wait_leaf, 0)

    def add(i, total):
        return total + gathered_ref[i, 8:16]

    total = lax.fori_loop(0, nleaf, add, jnp.zeros((8, KR), f32))
    sums[...] = total
    group_ref[g] = total

    def group_copy(d, slot):
        peer = lax.rem(g + d, ngroup)
        at = g if slot else peer
        return pltpu.make_async_remote_copy(
            src_ref=sums, dst_ref=group_ref.at[at], send_sem=group_send.at[d], recv_sem=group_recv.at[at],
            device_id=(peer, z), device_id_type=MESH)

    for d in range(1, ngroup):
        group_copy(d, True).start()
    for d in range(1, ngroup):
        group_copy(d, False).wait()


def params(**kw):
    return pltpu.CompilerParams(vmem_limit_bytes=48 * 1024 * 1024, **kw)


def per_device(
    right_sides,
    near_blocks,
    near_source,
    near_count,
    basis,
    leaf_source,
    leaf_coupling,
    leaf_transfer,
    cluster_source,
    cluster_coupling,
    cluster_transfer,
    group_coupling,
):
    leaves = near_blocks.shape[0]
    cpd = cluster_coupling.shape[0]
    ngroup, nleaf = lax.axis_size("group"), lax.axis_size("leaf")
    device = lax.axis_index(("group", "leaf"))
    window_start = (device - 1) * leaves
    axes = ("group", "leaf")
    size = ngroup * nleaf
    up = [(i, i + 1) for i in range(size - 1)]
    down = [(j, i) for i, j in up]

    x_before = lax.ppermute(right_sides, axes, up)
    x_after = lax.ppermute(right_sides, axes, down)

    basis3 = basis.reshape(leaves, K * LEAF // LANES, LANES)
    coef = pl.pallas_call(
        coef_kernel,
        out_shape=jax.ShapeDtypeStruct((leaves, K // 2, 2 * RHS), f32),
        in_specs=[VMEM, VMEM],
        out_specs=VMEM,
        compiler_params=params(),
        name="leaf_coefficients",
    )(right_sides, basis3)
    coef = coef.reshape(leaves, KR)
    coef_before = lax.ppermute(coef, axes, up)
    coef_after = lax.ppermute(coef, axes, down)

    wide = cpd * FAR1
    base = wide + 8
    assert ngroup <= 8 and cpd <= 8 and base + 8 <= LANES and leaves <= LANES
    small = jnp.concatenate(
        [
            cluster_coupling.reshape(wide, KK),
            jnp.pad(group_coupling.reshape(ngroup, KK), ((0, 8 - ngroup), (0, 0))),
            jnp.pad(cluster_transfer, ((0, 8 - cpd), (0, 0))),
        ],
        axis=0,
    )
    block = pl.pallas_call(
        functools.partial(up_kernel, base, cpd),
        out_shape=jax.ShapeDtypeStruct((16, KR), f32),
        in_specs=[VMEM] * 3,
        out_specs=VMEM,
        scratch_shapes=[
            pltpu.VMEM((KK, LANES), f32),
            pltpu.VMEM((KR, LANES), f32),
            pltpu.VMEM((KK, LANES), f32),
            pltpu.VMEM((KR, LANES), f32),
        ],
        compiler_params=params(),
        name="to_clusters",
    )(coef, leaf_transfer, small)

    gathered, group_sums = pl.pallas_call(
        functools.partial(exchange_kernel, nleaf, ngroup),
        out_shape=(
            jax.ShapeDtypeStruct((nleaf, 16, KR), f32),
            jax.ShapeDtypeStruct((ngroup, 8, KR), f32),
        ),
        in_specs=[VMEM],
        out_specs=(VMEM, VMEM),
        scratch_shapes=[
            pltpu.VMEM((8, KR), f32),
            pltpu.SemaphoreType.DMA((nleaf,)),
            pltpu.SemaphoreType.DMA((nleaf,)),
            pltpu.SemaphoreType.DMA((ngroup,)),
            pltpu.SemaphoreType.DMA((ngroup,)),
        ],
        compiler_params=params(collective_id=0, has_side_effects=True),
        name="exchange",
    )(block)

    rows = nleaf * 16
    padded = -(-rows // LANES) * LANES
    source_row = cluster_source // cpd * 16 + cluster_source % cpd
    cluster_idx = jnp.concatenate(
        [
            source_row.reshape(1, wide),
            padded + 8 * jnp.arange(ngroup, dtype=jnp.int32).reshape(1, ngroup),
            jnp.full((1, LANES - wide - ngroup), -1, jnp.int32),
        ],
        axis=1,
    )
    leaf_idx = (leaf_source - window_start).reshape(1, leaves * FAR0)
    coef_ext = jnp.concatenate([coef_before, coef, coef_after], axis=0)
    source_lanes = -(-3 * leaves // LANES) * LANES
    field = pl.pallas_call(
        functools.partial(down_kernel, base, cpd, ngroup),
        out_shape=jax.ShapeDtypeStruct((leaves, KR), f32),
        in_specs=[VMEM] * 9,
        out_specs=VMEM,
        scratch_shapes=[
            pltpu.VMEM((KK, LANES), f32),
            pltpu.VMEM((KR, source_lanes), f32),
            pltpu.VMEM((KK, LANES), f32),
            pltpu.VMEM((KK, leaves * FAR0), f32),
            pltpu.VMEM((KR, padded + LANES), f32),
            pltpu.VMEM((KR, leaves * FAR0), f32),
            pltpu.VMEM((KR, LANES), f32),
            pltpu.VMEM((KR, leaves * FAR0), f32),
            pltpu.VMEM((KR, LANES), f32),
        ],
        compiler_params=params(),
        name="from_clusters",
    )(
        coef_ext,
        coef,
        leaf_transfer,
        leaf_coupling.reshape(leaves * FAR0, KK),
        small,
        gathered.reshape(rows, KR),
        group_sums.reshape(ngroup * 8, KR),
        leaf_idx,
        cluster_idx,
    )
    field = field.reshape(leaves, K // 2, 2 * RHS).transpose(0, 2, 1)

    live = jnp.arange(NEAR, dtype=jnp.int32)[None, :] < near_count[:, None]
    near_idx = jnp.where(live, near_source - window_start, 3 * leaves).reshape(leaves * NEAR)
    whole = pl.BlockSpec((RHS, leaves * LEAF), lambda i: (0, 0))
    return pl.pallas_call(
        near_kernel,
        grid=(leaves // CHUNK,),
        out_shape=jax.ShapeDtypeStruct((RHS, leaves * LEAF), f32),
        in_specs=[
            SMEM,
            pl.BlockSpec((CHUNK, NEAR, LEAF * LEAF), lambda i: (i, 0, 0)),
            whole,
            whole,
            whole,
            pl.BlockSpec((CHUNK, K * LEAF // LANES, LANES), lambda i: (i, 0, 0)),
            pl.BlockSpec((CHUNK, 2 * RHS, K // 2), lambda i: (i, 0, 0)),
        ],
        out_specs=pl.BlockSpec((RHS, CHUNK * LEAF), lambda i: (0, i)),
        scratch_shapes=[
            pltpu.VMEM((3 * leaves + 1, 2 * RHS, LANES), bf16),
            pltpu.VMEM((3 * leaves + 1, 2 * RHS, LANES), bf16),
            pltpu.VMEM((4, 2 * LANES, LANES), bf16),
            pltpu.VMEM((CHUNK, 2 * RHS, 2 * LANES), f32),
        ],
        compiler_params=params(),
        name="near_and_sum",
    )(near_idx, near_blocks, x_before, right_sides, x_after, basis3, field)


def solution(mesh):
    split = P(("group", "leaf"))
    in_specs = (
        P(None, ("group", "leaf")),
        split,
        split,
        split,
        split,
        split,
        split,
        split,
        split,
        split,
        split,
        P("group"),
    )
    return jax.shard_map(
        per_device, mesh=mesh, in_specs=in_specs, out_specs=P(None, ("group", "leaf")), check_vma=False
    )
```

```python
import functools

import jax
import jax.numpy as jnp
from jax import lax
from jax.experimental import pallas as pl
from jax.experimental.pallas import tpu as pltpu
from jax.sharding import PartitionSpec as P

LEAF = 64
K = 32
RHS = 16
FAR0 = 8
FAR1 = 8
NEAR = 8
LANES = 128
KR = K * RHS
KK = K * K
CHUNK = 8

f32 = jnp.float32
bf16 = jnp.bfloat16
MESH = pl.DeviceIdType.MESH
VMEM = pl.BlockSpec(memory_space=pltpu.VMEM)
SMEM = pl.BlockSpec(memory_space=pltpu.SMEM)
NT = (((1,), (1,)), ((), ()))
NN = (((1,), (0,)), ((), ()))


def halves(value):
    high = value.astype(bf16)
    low = (value - high.astype(f32)).astype(bf16)
    return high, low


def mm(a, b, dims=NN):
    return lax.dot_general(a, b, dims, preferred_element_type=f32)


def pick(value, chosen):
    high, low = halves(value)
    return mm(high, chosen) + mm(low, chosen)


def iota(shape, dim):
    return lax.broadcasted_iota(jnp.int32, shape, dim)


def mask(condition):
    return jnp.where(condition, 1.0, 0.0).astype(bf16)


def doubled_pair(pair):
    first = iota(pair.shape, 1) < LEAF
    turned = pltpu.roll(pair, LEAF, 1)
    zero = jnp.zeros_like(pair)
    even = jnp.concatenate([jnp.where(first, pair, zero), jnp.where(first, zero, turned)], axis=0)
    odd = jnp.concatenate([jnp.where(first, turned, zero), jnp.where(first, zero, pair)], axis=0)
    return even, odd


def coef_kernel(x_ref, basis_ref, coef_ref):
    def step(p, carry):
        pair = x_ref[:, pl.ds(pl.multiple_of(p * LANES, LANES), LANES)]
        for side, doubled in enumerate(doubled_pair(pair)):
            xh, xl = halves(doubled)
            bh, bl = halves(basis_ref[2 * p + side])
            both = jnp.concatenate([bh, bl], axis=1)
            twice = jnp.concatenate([xh, xh], axis=1)
            coef_ref[2 * p + side] = mm(both, twice, NT) + mm(bh, xl, NT)
        return carry

    lax.fori_loop(0, basis_ref.shape[0] // 2, step, 0, unroll=4)


def turn(src, rows, dst_ref, lane):
    here = min(LANES, src.shape[0] - rows)
    for c in range(src.shape[1] // LANES):
        block = src[rows : rows + here, c * LANES : (c + 1) * LANES]
        if here < LANES:
            block = jnp.concatenate([block, jnp.zeros((LANES - here, LANES), f32)], axis=0)
        dst_ref[c * LANES : (c + 1) * LANES, lane : lane + LANES] = block.T


def small_products(at_ref, g_ref, out_ref, tiles, transposed=False):
    width = 8

    def step(i, carry):
        tile, kb = i // (K // width), i % (K // width)
        lanes = pl.ds(pl.multiple_of(tile * LANES, LANES), LANES)
        acc = [jnp.zeros((RHS, LANES), f32)] * width
        for l8 in range(0, K, 8):
            if transposed:
                at = [at_ref[pl.ds(pl.multiple_of(kb * 8, 8) + l * K, 8), lanes] for l in range(l8, l8 + 8)]
            else:
                at = [at_ref[pl.ds(pl.multiple_of(kb * 8 * K, 8 * K) + j * K + l8, 8), lanes] for j in range(width)]
            for i in range(8):
                g = g_ref[(l8 + i) * RHS : (l8 + i + 1) * RHS, lanes]
                for j in range(width):
                    row = at[i][j : j + 1] if transposed else at[j][i : i + 1]
                    acc[j] = acc[j] + row * g
        for j in range(width):
            start = pl.multiple_of(kb * (width * RHS) + j * RHS, RHS)
            out_ref[pl.ds(start, RHS), lanes] = acc[j]
        return carry

    lax.fori_loop(0, tiles * (K // width), step, 0)


def tree_kernel(base, cpd, nleaf, ngroup,
                idx_ref, x_ref, coef_ref, transfer_ref, small_ref, leaf_idx_ref, cluster_idx_ref, near_hbm, coupling_hbm,
                near_out, field_ref,
                near_ref, coupling_ref, xb, xa, coef_ext, block_ref, gathered_ref, group_ref, sums,
                xh_ref, xl_ref, place_ref, part_ref,
                et, ct, st, lt, gt, gl, work, lwork, small_g,
                local_sem, x_sem, coef_sem, leaf_send, leaf_recv, group_send, group_recv):
    leaves = transfer_ref.shape[0]
    per = leaves // cpd
    slots = leaves * FAR0
    wide = cpd * FAR1
    g, z = lax.axis_index("group"), lax.axis_index("leaf")
    size = nleaf * ngroup
    device = g * nleaf + z
    following, preceding = lax.rem(device + 1, size), lax.rem(device + size - 1, size)
    next_id = (following // nleaf, lax.rem(following, nleaf))
    prev_id = (preceding // nleaf, lax.rem(preceding, nleaf))
    has_next, has_prev = device < size - 1, device > 0
    cross_next = has_next & (z == nleaf - 1)
    cross_prev = has_prev & (z == 0)

    near_copy = pltpu.make_async_copy(near_hbm, near_ref, local_sem.at[0])
    coupling_copy = pltpu.make_async_copy(coupling_hbm, coupling_ref, local_sem.at[1])
    coupling_copy.start()
    near_copy.start()

    barrier = pltpu.get_barrier_semaphore()

    def greet_leaf(d, carry):
        pl.semaphore_signal(barrier, inc=1, device_id=(g, lax.rem(z + d, nleaf)), device_id_type=MESH)
        return carry

    def greet_group(d, carry):
        pl.semaphore_signal(barrier, inc=1, device_id=(lax.rem(g + d, ngroup), z), device_id_type=MESH)
        return carry

    lax.fori_loop(1, nleaf, greet_leaf, 0)
    lax.fori_loop(1, ngroup, greet_group, 0)

    @pl.when(cross_next)
    def _():
        pl.semaphore_signal(barrier, inc=1, device_id=next_id, device_id_type=MESH)

    @pl.when(cross_prev)
    def _():
        pl.semaphore_signal(barrier, inc=1, device_id=prev_id, device_id_type=MESH)

    def build(ref, part):
        def step(p, carry):
            pair = ref[:, pl.ds(pl.multiple_of(p * LANES, LANES), LANES)]
            for side, doubled in enumerate(doubled_pair(pair)):
                high, low = halves(doubled)
                xh_ref[part * leaves + 2 * p + side] = high
                xl_ref[part * leaves + 2 * p + side] = low
            return carry

        lax.fori_loop(0, leaves // 2, step, 0, unroll=4)

    turn(coef_ref, 0, ct, 0)
    turn(transfer_ref, 0, et, 0)
    turn(small_ref, 0, st, 0)
    coef_ext[leaves : 2 * leaves] = coef_ref[...]

    @pl.when(jnp.logical_not(has_prev))
    def _():
        xb[...] = jnp.zeros_like(xb)
        coef_ext[0:leaves] = jnp.zeros((leaves, KR), f32)

    @pl.when(jnp.logical_not(has_next))
    def _():
        xa[...] = jnp.zeros_like(xa)
        coef_ext[2 * leaves : 3 * leaves] = jnp.zeros((leaves, KR), f32)

    enough = nleaf + ngroup - 2
    crossing = cross_next | cross_prev

    @pl.when(crossing)
    def _():
        pl.semaphore_wait(barrier, enough + 1)

    @pl.when(jnp.logical_not(crossing))
    def _():
        pl.semaphore_wait(barrier, enough)

    def to_next(src, dst, sem):
        return pltpu.make_async_remote_copy(
            src_ref=src, dst_ref=dst, send_sem=sem.at[0], recv_sem=sem.at[2], device_id=next_id, device_id_type=MESH)

    def to_prev(src, dst, sem):
        return pltpu.make_async_remote_copy(
            src_ref=src, dst_ref=dst, send_sem=sem.at[1], recv_sem=sem.at[3], device_id=prev_id, device_id_type=MESH)

    moves = (
        (x_ref, xb, xa, x_sem),
        (coef_ref, coef_ext.at[pl.ds(0, leaves)], coef_ext.at[pl.ds(2 * leaves, leaves)], coef_sem),
    )

    @pl.when(has_next)
    def _():
        for src, before, after, sem in moves:
            to_next(src, before, sem).start()

    @pl.when(has_prev)
    def _():
        for src, before, after, sem in moves:
            to_prev(src, after, sem).start()

    def finish(move):
        src, before, after, sem = move

        @pl.when(has_next)
        def _():
            to_next(src, before, sem).wait_send()
            to_prev(src, after, sem).wait_recv()

        @pl.when(has_prev)
        def _():
            to_prev(src, after, sem).wait_send()
            to_next(src, before, sem).wait_recv()

    small_products(et, ct, work, 1)
    t, q = iota((LANES, LANES), 0), iota((LANES, LANES), 1)
    chosen = mask((q - base == t // per) & (t < leaves))
    small_g[...] = pick(work[...], chosen)
    small_products(st, small_g, work, 1)
    for c in range(KR // LANES):
        rows = slice(c * LANES, (c + 1) * LANES)
        block_ref[0:8, rows] = small_g[rows, :].T[base : base + 8]
        total = jnp.sum(work[rows, :].T[base : base + cpd], axis=0, keepdims=True)
        block_ref[8:16, rows] = jnp.broadcast_to(total, (8, LANES))

    def to_leaf(d):
        return pltpu.make_async_remote_copy(
            src_ref=block_ref, dst_ref=gathered_ref.at[z], send_sem=leaf_send.at[d], recv_sem=leaf_recv.at[z],
            device_id=(g, lax.rem(z + d, nleaf)), device_id_type=MESH)

    def from_leaf(d):
        peer = lax.rem(z + d, nleaf)
        return pltpu.make_async_remote_copy(
            src_ref=block_ref, dst_ref=gathered_ref.at[peer], send_sem=leaf_send.at[d], recv_sem=leaf_recv.at[peer],
            device_id=(g, peer), device_id_type=MESH)

    def start_leaf(d, carry):
        to_leaf(d).start()
        return carry

    def wait_leaf(d, carry):
        from_leaf(d).wait()
        return carry

    def group_copy(d, outgoing):
        peer = lax.rem(g + d, ngroup)
        at = g if outgoing else peer
        return pltpu.make_async_remote_copy(
            src_ref=sums, dst_ref=group_ref.at[at], send_sem=group_send.at[d], recv_sem=group_recv.at[at],
            device_id=(peer, z), device_id_type=MESH)

    lax.fori_loop(1, nleaf, start_leaf, 0)
    gathered_ref[z] = block_ref[...]

    build(x_ref, 1)
    xh_ref[3 * leaves] = jnp.zeros(xh_ref.shape[1:], bf16)
    xl_ref[3 * leaves] = jnp.zeros(xl_ref.shape[1:], bf16)
    row, col = iota((2 * LANES, LANES), 0), iota((2 * LANES, LANES), 1)
    for side in range(2):
        for half in range(2):
            place_ref[2 * side + half] = mask(col == side * LEAF + 2 * (row // NEAR) + half)
    coupling_copy.wait()
    for tile in range(slots // LANES):
        turn(coupling_ref, tile * LANES, lt, tile * LANES)
    finish(moves[0])
    build(xb, 0)
    build(xa, 2)
    near_copy.wait()

    slot_of_lane = iota((2 * RHS, 2 * LANES), 1) % NEAR

    def near_chunk(chunk, carry):
        for i in range(CHUNK):
            n = near_ref[chunk * CHUNK + i]
            rows = jnp.concatenate([n[:, c * LANES : (c + 1) * LANES] for c in range(LEAF // 2)], axis=0)
            nh, nl = halves(rows)
            weights = jnp.concatenate([nh, nl], axis=1)
            at = [idx_ref[(chunk * CHUNK + i) * NEAR + j] for j in range(NEAR)]
            xh = jnp.concatenate([xh_ref[s] for s in at], axis=0)
            xl = jnp.concatenate([xl_ref[s] for s in at], axis=0)
            full = mm(jnp.concatenate([xh, xh], axis=1), weights, NT) + mm(
                jnp.concatenate([xl, xl], axis=1), weights, NT
            )
            kept = full[: 2 * RHS]
            for j in range(1, NEAR):
                kept = jnp.where(slot_of_lane == j, full[j * 2 * RHS : (j + 1) * 2 * RHS], kept)
            part_ref[i] = kept
        total = jnp.zeros((CHUNK // 2 * RHS, LANES), f32)
        for side in range(2):
            for half in range(2):
                rows = jnp.concatenate(
                    [part_ref[2 * p + side, half * RHS : (half + 1) * RHS] for p in range(CHUNK // 2)], axis=0
                )
                total = total + pick(rows, place_ref[2 * side + half])
        for p in range(CHUNK // 2):
            lanes = pl.ds(pl.multiple_of(chunk * (CHUNK * LEAF) + p * LANES, LANES), LANES)
            near_out[:, lanes] = total[p * RHS : (p + 1) * RHS]
        return carry

    chunks = leaves // CHUNK
    lax.fori_loop(0, chunks // 2, near_chunk, 0)

    lax.fori_loop(1, nleaf, wait_leaf, 0)

    def add(i, total):
        return total + gathered_ref[i, 8:16]

    total = lax.fori_loop(0, nleaf, add, jnp.zeros((8, KR), f32))
    sums[...] = total
    group_ref[g] = total
    for d in range(1, ngroup):
        group_copy(d, True).start()

    lax.fori_loop(chunks // 2, chunks, near_chunk, 0)

    finish(moves[1])
    for part in range(-(-3 * leaves // LANES)):
        turn(coef_ext, part * LANES, ct, part * LANES)
    onehot = mask(iota((ct.shape[1], slots), 0) == leaf_idx_ref[...])
    gl[...] = pick(ct[...], onehot)
    small_products(lt, gl, lwork, slots // LANES)

    for d in range(1, ngroup):
        group_copy(d, False).wait()
    count = gt.shape[1]
    rows = nleaf * 16
    for part in range(-(-rows // LANES)):
        first = part * LANES // 16
        here = min(LANES // 16, nleaf - first)
        turn(gathered_ref[first : first + here].reshape(here * 16, KR), 0, gt, part * LANES)
    turn(group_ref[...].reshape(ngroup * 8, KR), 0, gt, count - LANES)
    onehot = mask(iota((count, LANES), 0) == cluster_idx_ref[...])
    small_g[...] = pick(gt[...], onehot)
    small_products(st, small_g, work, 1)
    a, b = t, q
    mine = (b >= base) & (b < base + cpd)
    top = mask((a >= wide) & (a < wide + ngroup) & mine)
    small_g[...] = pick(work[...], top)
    slot = mask((a < wide) & (b - base == a // FAR1))
    far = pick(work[...], slot)
    small_products(st, small_g, work, 1, transposed=True)
    spread = mask((a - base == b // per) & (b < leaves))
    small_g[...] = pick(far + work[...], spread)
    small_products(et, small_g, work, 1, transposed=True)
    gather = mask(iota((slots, LANES), 0) // FAR0 == iota((slots, LANES), 1))
    field = work[...] + pick(lwork[...], gather)
    for c in range(KR // LANES):
        rows_c = slice(c * LANES, (c + 1) * LANES)
        field_ref[:, rows_c] = field[rows_c].T[:leaves]


def sum_kernel(near_ref, basis_ref, field_ref, out_ref):
    first = iota((RHS, LANES), 1) < LEAF

    def step(p, carry):
        ends = []
        for side in range(2):
            i = 2 * p + side
            fh, fl = halves(field_ref[i])
            bh, bl = halves(basis_ref[i])
            wide = mm(jnp.concatenate([fh, fl], axis=0), jnp.concatenate([bh, bl], axis=1))
            both = wide[: 2 * RHS, :LANES] + wide[: 2 * RHS, LANES:] + wide[2 * RHS :, :LANES]
            ends.append((both[:RHS], both[RHS:]))
        straight = jnp.where(first, ends[0][0], ends[1][1])
        crossed = jnp.where(first, ends[1][0], ends[0][1])
        lanes = pl.ds(pl.multiple_of(p * LANES, LANES), LANES)
        out_ref[:, lanes] = near_ref[:, lanes] + straight + pltpu.roll(crossed, LEAF, 1)
        return carry

    lax.fori_loop(0, basis_ref.shape[0] // 2, step, 0, unroll=4)


def params(**kw):
    return pltpu.CompilerParams(vmem_limit_bytes=48 * 1024 * 1024, **kw)


def per_device(
    right_sides,
    near_blocks,
    near_source,
    near_count,
    basis,
    leaf_source,
    leaf_coupling,
    leaf_transfer,
    cluster_source,
    cluster_coupling,
    cluster_transfer,
    group_coupling,
):
    leaves = near_blocks.shape[0]
    cpd = cluster_coupling.shape[0]
    ngroup, nleaf = lax.axis_size("group"), lax.axis_size("leaf")
    device = lax.axis_index(("group", "leaf"))
    window_start = (device - 1) * leaves
    basis3 = basis.reshape(leaves, K * LEAF // LANES, LANES)
    coef = pl.pallas_call(
        coef_kernel,
        out_shape=jax.ShapeDtypeStruct((leaves, K // 2, 2 * RHS), f32),
        in_specs=[VMEM, VMEM],
        out_specs=VMEM,
        compiler_params=params(),
        name="leaf_coefficients",
    )(right_sides, basis3)
    coef = coef.reshape(leaves, KR)
    wide = cpd * FAR1
    base = wide + 8
    assert ngroup <= 8 and cpd <= 8 and base + 8 <= LANES and leaves <= LANES
    small = jnp.concatenate(
        [
            cluster_coupling.reshape(wide, KK),
            jnp.pad(group_coupling.reshape(ngroup, KK), ((0, 8 - ngroup), (0, 0))),
            jnp.pad(cluster_transfer, ((0, 8 - cpd), (0, 0))),
        ],
        axis=0,
    )
    rows = nleaf * 16
    padded = -(-rows // LANES) * LANES
    source_row = cluster_source // cpd * 16 + cluster_source % cpd
    cluster_idx = jnp.concatenate(
        [
            source_row.reshape(1, wide),
            padded + 8 * jnp.arange(ngroup, dtype=jnp.int32).reshape(1, ngroup),
            jnp.full((1, LANES - wide - ngroup), -1, jnp.int32),
        ],
        axis=1,
    )
    leaf_idx = (leaf_source - window_start).reshape(1, leaves * FAR0)
    source_lanes = -(-3 * leaves // LANES) * LANES
    slots = leaves * FAR0
    live = jnp.arange(NEAR, dtype=jnp.int32)[None, :] < near_count[:, None]
    near_idx = jnp.where(live, near_source - window_start, 3 * leaves).reshape(leaves * NEAR)
    near, field = pl.pallas_call(
        functools.partial(tree_kernel, base, cpd, nleaf, ngroup),
        out_shape=(
            jax.ShapeDtypeStruct((RHS, leaves * LEAF), f32),
            jax.ShapeDtypeStruct((leaves, KR), f32),
        ),
        in_specs=[SMEM] + [VMEM] * 6 + [pl.BlockSpec(memory_space=pl.ANY)] * 2,
        out_specs=(VMEM, VMEM),
        scratch_shapes=[
            pltpu.VMEM((leaves, NEAR, LEAF * LEAF), f32),
            pltpu.VMEM((slots, KK), f32),
            pltpu.VMEM((RHS, leaves * LEAF), f32),
            pltpu.VMEM((RHS, leaves * LEAF), f32),
            pltpu.VMEM((3 * leaves, KR), f32),
            pltpu.VMEM((16, KR), f32),
            pltpu.VMEM((nleaf, 16, KR), f32),
            pltpu.VMEM((ngroup, 8, KR), f32),
            pltpu.VMEM((8, KR), f32),
            pltpu.VMEM((3 * leaves + 1, 2 * RHS, LANES), bf16),
            pltpu.VMEM((3 * leaves + 1, 2 * RHS, LANES), bf16),
            pltpu.VMEM((4, 2 * LANES, LANES), bf16),
            pltpu.VMEM((CHUNK, 2 * RHS, 2 * LANES), f32),
            pltpu.VMEM((KK, LANES), f32),
            pltpu.VMEM((KR, source_lanes), f32),
            pltpu.VMEM((KK, LANES), f32),
            pltpu.VMEM((KK, slots), f32),
            pltpu.VMEM((KR, padded + LANES), f32),
            pltpu.VMEM((KR, slots), f32),
            pltpu.VMEM((KR, LANES), f32),
            pltpu.VMEM((KR, slots), f32),
            pltpu.VMEM((KR, LANES), f32),
            pltpu.SemaphoreType.DMA((2,)),
            pltpu.SemaphoreType.DMA((4,)),
            pltpu.SemaphoreType.DMA((4,)),
            pltpu.SemaphoreType.DMA((nleaf,)),
            pltpu.SemaphoreType.DMA((nleaf,)),
            pltpu.SemaphoreType.DMA((ngroup,)),
            pltpu.SemaphoreType.DMA((ngroup,)),
        ],
        compiler_params=params(collective_id=0, has_side_effects=True),
        name="tree_and_near",
    )(
        near_idx,
        right_sides,
        coef,
        leaf_transfer,
        small,
        leaf_idx,
        cluster_idx,
        near_blocks,
        leaf_coupling.reshape(slots, KK),
    )
    field = field.reshape(leaves, K // 2, 2 * RHS).transpose(0, 2, 1)
    return pl.pallas_call(
        sum_kernel,
        out_shape=jax.ShapeDtypeStruct((RHS, leaves * LEAF), f32),
        in_specs=[VMEM] * 3,
        out_specs=VMEM,
        compiler_params=params(),
        name="sum",
    )(near, basis3, field)


def solution(mesh):
    split = P(("group", "leaf"))
    in_specs = (
        P(None, ("group", "leaf")),
        split,
        split,
        split,
        split,
        split,
        split,
        split,
        split,
        split,
        split,
        P("group"),
    )
    return jax.shard_map(
        per_device, mesh=mesh, in_specs=in_specs, out_specs=P(None, ("group", "leaf")), check_vma=False
    )
```

```python
import functools

import jax
import jax.numpy as jnp
from jax import lax
from jax.experimental import pallas as pl
from jax.experimental.pallas import tpu as pltpu
from jax.sharding import PartitionSpec as P

LEAF = 64
K = 32
RHS = 16
FAR0 = 8
FAR1 = 8
NEAR = 8
LANES = 128
KR = K * RHS
KK = K * K
CHUNK = 8

f32 = jnp.float32
bf16 = jnp.bfloat16
MESH = pl.DeviceIdType.MESH
VMEM = pl.BlockSpec(memory_space=pltpu.VMEM)
SMEM = pl.BlockSpec(memory_space=pltpu.SMEM)
NT = (((1,), (1,)), ((), ()))
NN = (((1,), (0,)), ((), ()))
TN = (((0,), (0,)), ((), ()))


def halves(value):
    high = value.astype(bf16)
    low = (value - high.astype(f32)).astype(bf16)
    return high, low


def mm(a, b, dims=NN):
    return lax.dot_general(a, b, dims, preferred_element_type=f32)


def pick(value, chosen):
    high, low = halves(value)
    return mm(high, chosen) + mm(low, chosen)


def iota(shape, dim):
    return lax.broadcasted_iota(jnp.int32, shape, dim)


def mask(condition):
    return jnp.where(condition, 1.0, 0.0).astype(bf16)


def doubled_pair(pair):
    first = iota(pair.shape, 1) < LEAF
    turned = pltpu.roll(pair, LEAF, 1)
    zero = jnp.zeros_like(pair)
    even = jnp.concatenate([jnp.where(first, pair, zero), jnp.where(first, zero, turned)], axis=0)
    odd = jnp.concatenate([jnp.where(first, turned, zero), jnp.where(first, zero, pair)], axis=0)
    return even, odd


def coef_kernel(x_ref, basis_ref, coef_ref):
    def step(p, carry):
        pair = x_ref[:, pl.ds(pl.multiple_of(p * LANES, LANES), LANES)]
        for side, doubled in enumerate(doubled_pair(pair)):
            xh, xl = halves(doubled)
            bh, bl = halves(basis_ref[2 * p + side])
            both = jnp.concatenate([bh, bl], axis=1)
            twice = jnp.concatenate([xh, xh], axis=1)
            coef_ref[2 * p + side] = mm(both, twice, NT) + mm(bh, xl, NT)
        return carry

    lax.fori_loop(0, basis_ref.shape[0] // 2, step, 0, unroll=8)


def turn(src, rows, dst_ref, lane):
    here = min(LANES, src.shape[0] - rows)
    for c in range(src.shape[1] // LANES):
        block = src[rows : rows + here, c * LANES : (c + 1) * LANES]
        if here < LANES:
            block = jnp.concatenate([block, jnp.zeros((LANES - here, LANES), f32)], axis=0)
        dst_ref[c * LANES : (c + 1) * LANES, lane : lane + LANES] = block.T


def small_products(at_ref, g_ref, out_ref, tiles, transposed=False):
    width = 8

    def step(i, carry):
        tile, kb = i // (K // width), i % (K // width)
        lanes = pl.ds(pl.multiple_of(tile * LANES, LANES), LANES)
        acc = [jnp.zeros((RHS, LANES), f32)] * width
        for l8 in range(0, K, 8):
            if transposed:
                at = [at_ref[pl.ds(pl.multiple_of(kb * 8, 8) + l * K, 8), lanes] for l in range(l8, l8 + 8)]
            else:
                at = [at_ref[pl.ds(pl.multiple_of(kb * 8 * K, 8 * K) + j * K + l8, 8), lanes] for j in range(width)]
            for i in range(8):
                g = g_ref[(l8 + i) * RHS : (l8 + i + 1) * RHS, lanes]
                for j in range(width):
                    row = at[i][j : j + 1] if transposed else at[j][i : i + 1]
                    acc[j] = acc[j] + row * g
        for j in range(width):
            start = pl.multiple_of(kb * (width * RHS) + j * RHS, RHS)
            out_ref[pl.ds(start, RHS), lanes] = acc[j]
        return carry

    lax.fori_loop(0, tiles * (K // width), step, 0)


def tree_kernel(base, cpd, nleaf, ngroup,
                source_ref, count_ref, coef_ref, leaf_source_ref, cluster_source_ref,
                cluster_coupling_ref, group_coupling_ref, cluster_transfer_ref,
                x_hbm, transfer_hbm, near_hbm, coupling_hbm,
                near_out, field_ref,
                x_ref, transfer_ref, small_ref, near_ref, coupling_ref, xb, xa, coef_ext, block_ref, gathered_ref, group_ref, sums,
                xh_ref, xl_ref, place_ref, part_ref,
                et, ct, st, lt, gt, gl, work, lwork, small_g,
                local_sem, x_sem, coef_sem, leaf_send, leaf_recv, group_send, group_recv):
    leaves = transfer_ref.shape[0]
    per = leaves // cpd
    slots = leaves * FAR0
    wide = cpd * FAR1
    g, z = lax.axis_index("group"), lax.axis_index("leaf")
    size = nleaf * ngroup
    device = g * nleaf + z
    following, preceding = lax.rem(device + 1, size), lax.rem(device + size - 1, size)
    next_id = (following // nleaf, lax.rem(following, nleaf))
    prev_id = (preceding // nleaf, lax.rem(preceding, nleaf))
    has_next, has_prev = device < size - 1, device > 0
    cross_next = has_next & (z == nleaf - 1)
    cross_prev = has_prev & (z == 0)

    near_copy = pltpu.make_async_copy(near_hbm, near_ref, local_sem.at[0])
    coupling_copy = pltpu.make_async_copy(coupling_hbm, coupling_ref, local_sem.at[1])
    x_copy = pltpu.make_async_copy(x_hbm, x_ref, local_sem.at[2])
    transfer_copy = pltpu.make_async_copy(transfer_hbm, transfer_ref, local_sem.at[3])
    transfer_copy.start()
    x_copy.start()
    coupling_copy.start()
    near_copy.start()

    barrier = pltpu.get_barrier_semaphore()

    def greet_leaf(d, carry):
        pl.semaphore_signal(barrier, inc=1, device_id=(g, lax.rem(z + d, nleaf)), device_id_type=MESH)
        return carry

    def greet_group(d, carry):
        pl.semaphore_signal(barrier, inc=1, device_id=(lax.rem(g + d, ngroup), z), device_id_type=MESH)
        return carry

    lax.fori_loop(1, nleaf, greet_leaf, 0)
    lax.fori_loop(1, ngroup, greet_group, 0)

    @pl.when(cross_next)
    def _():
        pl.semaphore_signal(barrier, inc=1, device_id=next_id, device_id_type=MESH)

    @pl.when(cross_prev)
    def _():
        pl.semaphore_signal(barrier, inc=1, device_id=prev_id, device_id_type=MESH)

    def build(ref, part):
        def step(p, carry):
            pair = ref[:, pl.ds(pl.multiple_of(p * LANES, LANES), LANES)]
            for side, doubled in enumerate(doubled_pair(pair)):
                high, low = halves(doubled)
                xh_ref[part * leaves + 2 * p + side] = high
                xl_ref[part * leaves + 2 * p + side] = low
            return carry

        lax.fori_loop(0, leaves // 2, step, 0, unroll=8)

    turn(coef_ref, 0, ct, 0)
    small_ref[...] = jnp.zeros_like(small_ref)
    small_ref[0:wide] = cluster_coupling_ref[...]
    small_ref[wide : wide + ngroup] = group_coupling_ref[...]
    small_ref[base : base + cpd] = cluster_transfer_ref[...]
    turn(small_ref, 0, st, 0)
    transfer_copy.wait()
    turn(transfer_ref, 0, et, 0)
    coef_ext[leaves : 2 * leaves] = coef_ref[...]

    @pl.when(jnp.logical_not(has_prev))
    def _():
        xb[...] = jnp.zeros_like(xb)
        coef_ext[0:leaves] = jnp.zeros((leaves, KR), f32)

    @pl.when(jnp.logical_not(has_next))
    def _():
        xa[...] = jnp.zeros_like(xa)
        coef_ext[2 * leaves : 3 * leaves] = jnp.zeros((leaves, KR), f32)

    enough = nleaf + ngroup - 2
    crossing = cross_next | cross_prev

    @pl.when(crossing)
    def _():
        pl.semaphore_wait(barrier, enough + 1)

    @pl.when(jnp.logical_not(crossing))
    def _():
        pl.semaphore_wait(barrier, enough)

    def to_next(src, dst, sem):
        return pltpu.make_async_remote_copy(
            src_ref=src, dst_ref=dst, send_sem=sem.at[0], recv_sem=sem.at[2], device_id=next_id, device_id_type=MESH)

    def to_prev(src, dst, sem):
        return pltpu.make_async_remote_copy(
            src_ref=src, dst_ref=dst, send_sem=sem.at[1], recv_sem=sem.at[3], device_id=prev_id, device_id_type=MESH)

    moves = (
        (x_hbm, xb, xa, x_sem),
        (coef_ref, coef_ext.at[pl.ds(0, leaves)], coef_ext.at[pl.ds(2 * leaves, leaves)], coef_sem),
    )

    @pl.when(has_next)
    def _():
        for src, before, after, sem in moves:
            to_next(src, before, sem).start()

    @pl.when(has_prev)
    def _():
        for src, before, after, sem in moves:
            to_prev(src, after, sem).start()

    def finish(move):
        src, before, after, sem = move

        @pl.when(has_next)
        def _():
            to_next(src, before, sem).wait_send()
            to_prev(src, after, sem).wait_recv()

        @pl.when(has_prev)
        def _():
            to_prev(src, after, sem).wait_send()
            to_next(src, before, sem).wait_recv()

    small_products(et, ct, work, 1)
    t, q = iota((LANES, LANES), 0), iota((LANES, LANES), 1)
    chosen = mask((q - base == t // per) & (t < leaves))
    small_g[...] = pick(work[...], chosen)
    small_products(st, small_g, work, 1)
    for c in range(KR // LANES):
        rows = slice(c * LANES, (c + 1) * LANES)
        block_ref[0:8, rows] = small_g[rows, :].T[base : base + 8]
        total = jnp.sum(work[rows, :].T[base : base + cpd], axis=0, keepdims=True)
        block_ref[8:16, rows] = jnp.broadcast_to(total, (8, LANES))

    def to_leaf(d):
        return pltpu.make_async_remote_copy(
            src_ref=block_ref, dst_ref=gathered_ref.at[z], send_sem=leaf_send.at[d], recv_sem=leaf_recv.at[z],
            device_id=(g, lax.rem(z + d, nleaf)), device_id_type=MESH)

    def from_leaf(d):
        peer = lax.rem(z + d, nleaf)
        return pltpu.make_async_remote_copy(
            src_ref=block_ref, dst_ref=gathered_ref.at[peer], send_sem=leaf_send.at[d], recv_sem=leaf_recv.at[peer],
            device_id=(g, peer), device_id_type=MESH)

    def start_leaf(d, carry):
        to_leaf(d).start()
        return carry

    def wait_leaf(d, carry):
        from_leaf(d).wait()
        return carry

    def group_copy(d, outgoing):
        peer = lax.rem(g + d, ngroup)
        at = g if outgoing else peer
        return pltpu.make_async_remote_copy(
            src_ref=sums, dst_ref=group_ref.at[at], send_sem=group_send.at[d], recv_sem=group_recv.at[at],
            device_id=(peer, z), device_id_type=MESH)

    lax.fori_loop(1, nleaf, start_leaf, 0)
    gathered_ref[z] = block_ref[...]

    x_copy.wait()
    build(x_ref, 1)
    xh_ref[3 * leaves] = jnp.zeros(xh_ref.shape[1:], bf16)
    xl_ref[3 * leaves] = jnp.zeros(xl_ref.shape[1:], bf16)
    row, col = iota((2 * LANES, LANES), 0), iota((2 * LANES, LANES), 1)
    for side in range(2):
        for half in range(2):
            place_ref[2 * side + half] = mask(col == side * LEAF + 2 * (row // NEAR) + half)
    coupling_copy.wait()
    for tile in range(slots // LANES):
        turn(coupling_ref, tile * LANES, lt, tile * LANES)
    finish(moves[0])
    build(xb, 0)
    build(xa, 2)
    near_copy.wait()

    slot_of_lane = iota((2 * RHS, 2 * LANES), 1) % NEAR

    def near_chunk(chunk, carry):
        for i in range(CHUNK):
            n = near_ref[chunk * CHUNK + i]
            rows = jnp.concatenate([n[:, c * LANES : (c + 1) * LANES] for c in range(LEAF // 2)], axis=0)
            nh, nl = halves(rows)
            weights = jnp.concatenate([nh, nl], axis=1)
            leaf = chunk * CHUNK + i
            live = count_ref[leaf]
            at = [
                jnp.where(j < live, source_ref[j, leaf] - (device - 1) * leaves, 3 * leaves) for j in range(NEAR)
            ]
            xh = jnp.concatenate([xh_ref[s] for s in at], axis=0)
            xl = jnp.concatenate([xl_ref[s] for s in at], axis=0)
            full = mm(jnp.concatenate([xh, xh], axis=1), weights, NT) + mm(
                jnp.concatenate([xl, xl], axis=1), weights, NT
            )
            kept = full[: 2 * RHS]
            for j in range(1, NEAR):
                kept = jnp.where(slot_of_lane == j, full[j * 2 * RHS : (j + 1) * 2 * RHS], kept)
            part_ref[i] = kept
        total = jnp.zeros((CHUNK // 2 * RHS, LANES), f32)
        for side in range(2):
            for half in range(2):
                rows = jnp.concatenate(
                    [part_ref[2 * p + side, half * RHS : (half + 1) * RHS] for p in range(CHUNK // 2)], axis=0
                )
                total = total + pick(rows, place_ref[2 * side + half])
        for p in range(CHUNK // 2):
            lanes = pl.ds(pl.multiple_of(chunk * (CHUNK * LEAF) + p * LANES, LANES), LANES)
            near_out[:, lanes] = total[p * RHS : (p + 1) * RHS]
        return carry

    chunks = leaves // CHUNK
    lax.fori_loop(0, chunks // 2, near_chunk, 0)

    lax.fori_loop(1, nleaf, wait_leaf, 0)

    def add(i, total):
        return total + gathered_ref[i, 8:16]

    total = lax.fori_loop(0, nleaf, add, jnp.zeros((8, KR), f32))
    sums[...] = total
    group_ref[g] = total
    for d in range(1, ngroup):
        group_copy(d, True).start()

    lax.fori_loop(chunks // 2, chunks, near_chunk, 0)

    finish(moves[1])
    for part in range(-(-3 * leaves // LANES)):
        turn(coef_ext, part * LANES, ct, part * LANES)
    local = (leaf_source_ref[...] - (device - 1) * leaves).astype(f32)
    lane = iota((leaves, slots), 1)
    expanded = mm(local.astype(bf16), mask(lane // FAR0 == iota((leaves, slots), 0)))
    lane = iota((FAR0, slots), 1)
    wanted = jnp.sum(jnp.where(lane % FAR0 == iota((FAR0, slots), 0), expanded, 0.0), axis=0, keepdims=True)
    onehot = mask(iota((ct.shape[1], slots), 0) == wanted.astype(jnp.int32))
    gl[...] = pick(ct[...], onehot)
    small_products(lt, gl, lwork, slots // LANES)

    for d in range(1, ngroup):
        group_copy(d, False).wait()
    count = gt.shape[1]
    rows = nleaf * 16
    for part in range(-(-rows // LANES)):
        first = part * LANES // 16
        here = min(LANES // 16, nleaf - first)
        turn(gathered_ref[first : first + here].reshape(here * 16, KR), 0, gt, part * LANES)
    turn(group_ref[...].reshape(ngroup * 8, KR), 0, gt, count - LANES)
    sources = cluster_source_ref[...]
    lane = iota((1, LANES), 1)
    wanted = jnp.full((1, LANES), -1, jnp.int32)
    for u in range(cpd):
        for j in range(FAR1):
            wanted = jnp.where(lane == u * FAR1 + j, sources[u : u + 1, j : j + 1], wanted)
    wanted = jnp.where(wanted >= 0, wanted // cpd * 16 + wanted % cpd, -1)
    wanted = jnp.where((lane >= wide) & (lane < wide + ngroup), count - LANES + 8 * (lane - wide), wanted)
    onehot = mask(iota((count, LANES), 0) == wanted)
    small_g[...] = pick(gt[...], onehot)
    small_products(st, small_g, work, 1)
    a, b = t, q
    mine = (b >= base) & (b < base + cpd)
    top = mask((a >= wide) & (a < wide + ngroup) & mine)
    small_g[...] = pick(work[...], top)
    slot = mask((a < wide) & (b - base == a // FAR1))
    far = pick(work[...], slot)
    small_products(st, small_g, work, 1, transposed=True)
    spread = mask((a - base == b // per) & (b < leaves))
    small_g[...] = pick(far + work[...], spread)
    small_products(et, small_g, work, 1, transposed=True)
    gather = mask(iota((slots, LANES), 0) // FAR0 == iota((slots, LANES), 1))
    field = work[...] + pick(lwork[...], gather)
    for c in range(KR // LANES):
        rows_c = slice(c * LANES, (c + 1) * LANES)
        field_ref[:, rows_c] = field[rows_c].T[:leaves]


def sum_kernel(near_ref, basis_ref, field_ref, out_ref):
    first = iota((RHS, LANES), 1) < LEAF

    def step(p, carry):
        ends = []
        for side in range(2):
            i = 2 * p + side
            fh, fl = halves(field_ref[i])
            bh, bl = halves(basis_ref[i])
            wide = mm(jnp.concatenate([fh, fl], axis=1), jnp.concatenate([bh, bl], axis=1), TN)
            both = wide[: 2 * RHS, :LANES] + wide[: 2 * RHS, LANES:] + wide[2 * RHS :, :LANES]
            ends.append((both[:RHS], both[RHS:]))
        straight = jnp.where(first, ends[0][0], ends[1][1])
        crossed = jnp.where(first, ends[1][0], ends[0][1])
        lanes = pl.ds(pl.multiple_of(p * LANES, LANES), LANES)
        out_ref[:, lanes] = near_ref[:, lanes] + straight + pltpu.roll(crossed, LEAF, 1)
        return carry

    lax.fori_loop(0, basis_ref.shape[0] // 2, step, 0, unroll=8)


def params(mib=48, **kw):
    return pltpu.CompilerParams(vmem_limit_bytes=mib * 1024 * 1024, **kw)


def per_device(
    right_sides,
    near_blocks,
    near_source,
    near_count,
    basis,
    leaf_source,
    leaf_coupling,
    leaf_transfer,
    cluster_source,
    cluster_coupling,
    cluster_transfer,
    group_coupling,
):
    leaves = near_blocks.shape[0]
    cpd = cluster_coupling.shape[0]
    ngroup, nleaf = lax.axis_size("group"), lax.axis_size("leaf")
    basis3 = basis.reshape(leaves, K * LEAF // LANES, LANES)
    coef = pl.pallas_call(
        coef_kernel,
        out_shape=jax.ShapeDtypeStruct((leaves, K // 2, 2 * RHS), f32),
        in_specs=[VMEM, VMEM],
        out_specs=VMEM,
        compiler_params=params(),
        name="leaf_coefficients",
    )(right_sides, basis3)
    coef = coef.reshape(leaves, KR)
    wide = cpd * FAR1
    base = wide + 8
    assert ngroup <= 8 and cpd <= 8 and base + 8 <= LANES and leaves <= LANES
    rows = nleaf * 16
    padded = -(-rows // LANES) * LANES
    source_lanes = -(-3 * leaves // LANES) * LANES
    slots = leaves * FAR0
    near, field = pl.pallas_call(
        functools.partial(tree_kernel, base, cpd, nleaf, ngroup),
        out_shape=(
            jax.ShapeDtypeStruct((RHS, leaves * LEAF), f32),
            jax.ShapeDtypeStruct((leaves, KR), f32),
        ),
        in_specs=[SMEM] * 2 + [VMEM] * 6 + [pl.BlockSpec(memory_space=pl.ANY)] * 4,
        out_specs=(VMEM, VMEM),
        scratch_shapes=[
            pltpu.VMEM((RHS, leaves * LEAF), f32),
            pltpu.VMEM((leaves, KK), f32),
            pltpu.VMEM((base + 8, KK), f32),
            pltpu.VMEM((leaves, NEAR, LEAF * LEAF), f32),
            pltpu.VMEM((slots, KK), f32),
            pltpu.VMEM((RHS, leaves * LEAF), f32),
            pltpu.VMEM((RHS, leaves * LEAF), f32),
            pltpu.VMEM((3 * leaves, KR), f32),
            pltpu.VMEM((16, KR), f32),
            pltpu.VMEM((nleaf, 16, KR), f32),
            pltpu.VMEM((ngroup, 8, KR), f32),
            pltpu.VMEM((8, KR), f32),
            pltpu.VMEM((3 * leaves + 1, 2 * RHS, LANES), bf16),
            pltpu.VMEM((3 * leaves + 1, 2 * RHS, LANES), bf16),
            pltpu.VMEM((4, 2 * LANES, LANES), bf16),
            pltpu.VMEM((CHUNK, 2 * RHS, 2 * LANES), f32),
            pltpu.VMEM((KK, LANES), f32),
            pltpu.VMEM((KR, source_lanes), f32),
            pltpu.VMEM((KK, LANES), f32),
            pltpu.VMEM((KK, slots), f32),
            pltpu.VMEM((KR, padded + LANES), f32),
            pltpu.VMEM((KR, slots), f32),
            pltpu.VMEM((KR, LANES), f32),
            pltpu.VMEM((KR, slots), f32),
            pltpu.VMEM((KR, LANES), f32),
            pltpu.SemaphoreType.DMA((4,)),
            pltpu.SemaphoreType.DMA((4,)),
            pltpu.SemaphoreType.DMA((4,)),
            pltpu.SemaphoreType.DMA((nleaf,)),
            pltpu.SemaphoreType.DMA((nleaf,)),
            pltpu.SemaphoreType.DMA((ngroup,)),
            pltpu.SemaphoreType.DMA((ngroup,)),
        ],
        compiler_params=params(63, collective_id=0, has_side_effects=True),
        name="tree_and_near",
    )(
        near_source.T,
        near_count,
        coef,
        leaf_source.T,
        cluster_source,
        cluster_coupling.reshape(wide, KK),
        group_coupling.reshape(ngroup, KK),
        cluster_transfer,
        right_sides,
        leaf_transfer,
        near_blocks,
        leaf_coupling.reshape(slots, KK),
    )
    field = field.reshape(leaves, K // 2, 2 * RHS)
    return pl.pallas_call(
        sum_kernel,
        out_shape=jax.ShapeDtypeStruct((RHS, leaves * LEAF), f32),
        in_specs=[VMEM] * 3,
        out_specs=VMEM,
        compiler_params=params(),
        name="sum",
    )(near, basis3, field)


def solution(mesh):
    split = P(("group", "leaf"))
    in_specs = (
        P(None, ("group", "leaf")),
        split,
        split,
        split,
        split,
        split,
        split,
        split,
        split,
        split,
        split,
        P("group"),
    )
    return jax.shard_map(
        per_device, mesh=mesh, in_specs=in_specs, out_specs=P(None, ("group", "leaf")), check_vma=False
    )
```

```python
import functools

import jax
import jax.numpy as jnp
from jax import lax
from jax.experimental import pallas as pl
from jax.experimental.pallas import tpu as pltpu
from jax.sharding import PartitionSpec as P

LEAF = 64
K = 32
RHS = 16
FAR0 = 8
FAR1 = 8
NEAR = 8
LANES = 128
KR = K * RHS
KK = K * K
CHUNK = 8

f32 = jnp.float32
bf16 = jnp.bfloat16
MESH = pl.DeviceIdType.MESH
VMEM = pl.BlockSpec(memory_space=pltpu.VMEM)
SMEM = pl.BlockSpec(memory_space=pltpu.SMEM)
NT = (((1,), (1,)), ((), ()))
NN = (((1,), (0,)), ((), ()))
TN = (((0,), (0,)), ((), ()))


def halves(value):
    high = value.astype(bf16)
    low = (value - high.astype(f32)).astype(bf16)
    return high, low


def mm(a, b, dims=NN):
    return lax.dot_general(a, b, dims, preferred_element_type=f32)


def pick(value, chosen):
    high, low = halves(value)
    return mm(high, chosen) + mm(low, chosen)


def iota(shape, dim):
    return lax.broadcasted_iota(jnp.int32, shape, dim)


def mask(condition):
    return jnp.where(condition, 1.0, 0.0).astype(bf16)


def doubled_pair(pair):
    first = iota(pair.shape, 1) < LEAF
    turned = pltpu.roll(pair, LEAF, 1)
    zero = jnp.zeros_like(pair)
    even = jnp.concatenate([jnp.where(first, pair, zero), jnp.where(first, zero, turned)], axis=0)
    odd = jnp.concatenate([jnp.where(first, turned, zero), jnp.where(first, zero, pair)], axis=0)
    return even, odd


def coef_kernel(x_ref, basis_ref, coef_ref):
    def step(p, carry):
        pair = x_ref[:, pl.ds(pl.multiple_of(p * LANES, LANES), LANES)]
        for side, doubled in enumerate(doubled_pair(pair)):
            xh, xl = halves(doubled)
            bh, bl = halves(basis_ref[2 * p + side])
            both = jnp.concatenate([bh, bl], axis=1)
            twice = jnp.concatenate([xh, xh], axis=1)
            coef_ref[2 * p + side] = mm(both, twice, NT) + mm(bh, xl, NT)
        return carry

    lax.fori_loop(0, basis_ref.shape[0] // 2, step, 0, unroll=8)


def turn(src, rows, dst_ref, lane):
    here = min(LANES, src.shape[0] - rows)
    for c in range(src.shape[1] // LANES):
        block = src[rows : rows + here, c * LANES : (c + 1) * LANES]
        if here < LANES:
            block = jnp.concatenate([block, jnp.zeros((LANES - here, LANES), f32)], axis=0)
        dst_ref[c * LANES : (c + 1) * LANES, lane : lane + LANES] = block.T


def small_products(at_ref, g_ref, out_ref, tiles, transposed=False):
    width = 8

    def step(i, carry):
        tile, kb = i // (K // width), i % (K // width)
        lanes = pl.ds(pl.multiple_of(tile * LANES, LANES), LANES)
        acc = [jnp.zeros((RHS, LANES), f32)] * width
        for l8 in range(0, K, 8):
            if transposed:
                at = [at_ref[pl.ds(pl.multiple_of(kb * 8, 8) + l * K, 8), lanes] for l in range(l8, l8 + 8)]
            else:
                at = [at_ref[pl.ds(pl.multiple_of(kb * 8 * K, 8 * K) + j * K + l8, 8), lanes] for j in range(width)]
            for i in range(8):
                g = g_ref[(l8 + i) * RHS : (l8 + i + 1) * RHS, lanes]
                for j in range(width):
                    row = at[i][j : j + 1] if transposed else at[j][i : i + 1]
                    acc[j] = acc[j] + row * g
        for j in range(width):
            start = pl.multiple_of(kb * (width * RHS) + j * RHS, RHS)
            out_ref[pl.ds(start, RHS), lanes] = acc[j]
        return carry

    lax.fori_loop(0, tiles * (K // width), step, 0)


def tree_kernel(base, cpd, nleaf, ngroup,
                source_ref, count_ref, basis_in_ref, leaf_source_ref, cluster_source_ref,
                cluster_coupling_ref, group_coupling_ref, cluster_transfer_ref,
                x_hbm, transfer_hbm, near_hbm, coupling_hbm,
                near_out, field_ref, basis_ref,
                coef_blocks, coef_ref, x_ref, transfer_ref, small_ref, near_ref, coupling_ref, xb, xa, coef_ext, block_ref, gathered_ref, group_ref, sums,
                xh_ref, xl_ref, place_ref, part_ref,
                et, ct, st, lt, gt, gl, work, lwork, small_g,
                local_sem, x_sem, coef_sem, leaf_send, leaf_recv, group_send, group_recv):
    leaves = transfer_ref.shape[0]
    per = leaves // cpd
    slots = leaves * FAR0
    wide = cpd * FAR1
    g, z = lax.axis_index("group"), lax.axis_index("leaf")
    size = nleaf * ngroup
    device = g * nleaf + z
    following, preceding = lax.rem(device + 1, size), lax.rem(device + size - 1, size)
    next_id = (following // nleaf, lax.rem(following, nleaf))
    prev_id = (preceding // nleaf, lax.rem(preceding, nleaf))
    has_next, has_prev = device < size - 1, device > 0
    cross_next = has_next & (z == nleaf - 1)
    cross_prev = has_prev & (z == 0)

    near_copy = pltpu.make_async_copy(near_hbm, near_ref, local_sem.at[0])
    coupling_copy = pltpu.make_async_copy(coupling_hbm, coupling_ref, local_sem.at[1])
    x_copy = pltpu.make_async_copy(x_hbm, x_ref, local_sem.at[2])
    transfer_copy = pltpu.make_async_copy(transfer_hbm, transfer_ref, local_sem.at[3])
    x_copy.start()
    transfer_copy.start()
    coupling_copy.start()
    near_copy.start()

    barrier = pltpu.get_barrier_semaphore()

    def greet_leaf(d, carry):
        pl.semaphore_signal(barrier, inc=1, device_id=(g, lax.rem(z + d, nleaf)), device_id_type=MESH)
        return carry

    def greet_group(d, carry):
        pl.semaphore_signal(barrier, inc=1, device_id=(lax.rem(g + d, ngroup), z), device_id_type=MESH)
        return carry

    lax.fori_loop(1, nleaf, greet_leaf, 0)
    lax.fori_loop(1, ngroup, greet_group, 0)

    @pl.when(cross_next)
    def _():
        pl.semaphore_signal(barrier, inc=1, device_id=next_id, device_id_type=MESH)

    @pl.when(cross_prev)
    def _():
        pl.semaphore_signal(barrier, inc=1, device_id=prev_id, device_id_type=MESH)

    def build(ref, part):
        def step(p, carry):
            pair = ref[:, pl.ds(pl.multiple_of(p * LANES, LANES), LANES)]
            for side, doubled in enumerate(doubled_pair(pair)):
                high, low = halves(doubled)
                xh_ref[part * leaves + 2 * p + side] = high
                xl_ref[part * leaves + 2 * p + side] = low
            return carry

        lax.fori_loop(0, leaves // 2, step, 0, unroll=8)


    @pl.when(jnp.logical_not(has_prev))
    def _():
        xb[...] = jnp.zeros_like(xb)
        coef_ext[0:leaves] = jnp.zeros((leaves, KR), f32)

    @pl.when(jnp.logical_not(has_next))
    def _():
        xa[...] = jnp.zeros_like(xa)
        coef_ext[2 * leaves : 3 * leaves] = jnp.zeros((leaves, KR), f32)

    enough = nleaf + ngroup - 2
    crossing = cross_next | cross_prev

    @pl.when(crossing)
    def _():
        pl.semaphore_wait(barrier, enough + 1)

    @pl.when(jnp.logical_not(crossing))
    def _():
        pl.semaphore_wait(barrier, enough)

    def to_next(src, dst, sem):
        return pltpu.make_async_remote_copy(
            src_ref=src, dst_ref=dst, send_sem=sem.at[0], recv_sem=sem.at[2], device_id=next_id, device_id_type=MESH)

    def to_prev(src, dst, sem):
        return pltpu.make_async_remote_copy(
            src_ref=src, dst_ref=dst, send_sem=sem.at[1], recv_sem=sem.at[3], device_id=prev_id, device_id_type=MESH)

    moves = (
        (x_hbm, xb, xa, x_sem),
        (coef_ref, coef_ext.at[pl.ds(0, leaves)], coef_ext.at[pl.ds(2 * leaves, leaves)], coef_sem),
    )

    def send(move):
        src, before, after, sem = move

        @pl.when(has_next)
        def _():
            to_next(src, before, sem).start()

        @pl.when(has_prev)
        def _():
            to_prev(src, after, sem).start()

    send(moves[0])

    def finish(move):
        src, before, after, sem = move

        @pl.when(has_next)
        def _():
            to_next(src, before, sem).wait_send()
            to_prev(src, after, sem).wait_recv()

        @pl.when(has_prev)
        def _():
            to_prev(src, after, sem).wait_send()
            to_next(src, before, sem).wait_recv()

    for c in range(K * LEAF // LANES):
        basis_ref[:, c, :] = basis_in_ref[:, c * LANES : (c + 1) * LANES]
    x_copy.wait()
    coef_kernel(x_ref, basis_ref, coef_blocks)
    ct[...] = jnp.zeros_like(ct)
    for c in range(K // 2):
        ct[c * 2 * RHS : (c + 1) * 2 * RHS, 0:leaves] = coef_blocks[:, c, :].T
    for c in range(KR // LANES):
        rows = slice(c * LANES, (c + 1) * LANES)
        coef_ref[:, rows] = ct[rows, 0:LANES].T[:leaves]
    coef_ext[leaves : 2 * leaves] = coef_ref[...]
    send(moves[1])

    small_ref[...] = jnp.zeros_like(small_ref)
    small_ref[0:wide] = cluster_coupling_ref[...]
    small_ref[wide : wide + ngroup] = group_coupling_ref[...]
    small_ref[base : base + cpd] = cluster_transfer_ref[...]
    turn(small_ref, 0, st, 0)
    transfer_copy.wait()
    turn(transfer_ref, 0, et, 0)
    small_products(et, ct, work, 1)
    t, q = iota((LANES, LANES), 0), iota((LANES, LANES), 1)
    chosen = mask((q - base == t // per) & (t < leaves))
    small_g[...] = pick(work[...], chosen)
    small_products(st, small_g, work, 1)
    for c in range(KR // LANES):
        rows = slice(c * LANES, (c + 1) * LANES)
        block_ref[0:8, rows] = small_g[rows, :].T[base : base + 8]
        total = jnp.sum(work[rows, :].T[base : base + cpd], axis=0, keepdims=True)
        block_ref[8:16, rows] = jnp.broadcast_to(total, (8, LANES))

    def to_leaf(d):
        return pltpu.make_async_remote_copy(
            src_ref=block_ref, dst_ref=gathered_ref.at[z], send_sem=leaf_send.at[d], recv_sem=leaf_recv.at[z],
            device_id=(g, lax.rem(z + d, nleaf)), device_id_type=MESH)

    def from_leaf(d):
        peer = lax.rem(z + d, nleaf)
        return pltpu.make_async_remote_copy(
            src_ref=block_ref, dst_ref=gathered_ref.at[peer], send_sem=leaf_send.at[d], recv_sem=leaf_recv.at[peer],
            device_id=(g, peer), device_id_type=MESH)

    def start_leaf(d, carry):
        to_leaf(d).start()
        return carry

    def wait_leaf(d, carry):
        from_leaf(d).wait()
        return carry

    def group_copy(d, outgoing):
        peer = lax.rem(g + d, ngroup)
        at = g if outgoing else peer
        return pltpu.make_async_remote_copy(
            src_ref=sums, dst_ref=group_ref.at[at], send_sem=group_send.at[d], recv_sem=group_recv.at[at],
            device_id=(peer, z), device_id_type=MESH)

    lax.fori_loop(1, nleaf, start_leaf, 0)
    gathered_ref[z] = block_ref[...]

    build(x_ref, 1)
    xh_ref[3 * leaves] = jnp.zeros(xh_ref.shape[1:], bf16)
    xl_ref[3 * leaves] = jnp.zeros(xl_ref.shape[1:], bf16)
    row, col = iota((2 * LANES, LANES), 0), iota((2 * LANES, LANES), 1)
    for side in range(2):
        for half in range(2):
            place_ref[2 * side + half] = mask(col == side * LEAF + 2 * (row // NEAR) + half)
    coupling_copy.wait()
    for tile in range(slots // LANES):
        turn(coupling_ref, tile * LANES, lt, tile * LANES)
    finish(moves[0])
    build(xb, 0)
    build(xa, 2)
    near_copy.wait()

    slot_of_lane = iota((2 * RHS, 2 * LANES), 1) % NEAR

    def near_chunk(chunk, carry):
        for i in range(CHUNK):
            n = near_ref[chunk * CHUNK + i]
            rows = jnp.concatenate([n[:, c * LANES : (c + 1) * LANES] for c in range(LEAF // 2)], axis=0)
            nh, nl = halves(rows)
            weights = jnp.concatenate([nh, nl], axis=1)
            leaf = chunk * CHUNK + i
            live = count_ref[leaf]
            at = [
                jnp.where(j < live, source_ref[j, leaf] - (device - 1) * leaves, 3 * leaves) for j in range(NEAR)
            ]
            xh = jnp.concatenate([xh_ref[s] for s in at], axis=0)
            xl = jnp.concatenate([xl_ref[s] for s in at], axis=0)
            full = mm(jnp.concatenate([xh, xh], axis=1), weights, NT) + mm(
                jnp.concatenate([xl, xl], axis=1), weights, NT
            )
            kept = full[: 2 * RHS]
            for j in range(1, NEAR):
                kept = jnp.where(slot_of_lane == j, full[j * 2 * RHS : (j + 1) * 2 * RHS], kept)
            part_ref[i] = kept
        total = jnp.zeros((CHUNK // 2 * RHS, LANES), f32)
        for side in range(2):
            for half in range(2):
                rows = jnp.concatenate(
                    [part_ref[2 * p + side, half * RHS : (half + 1) * RHS] for p in range(CHUNK // 2)], axis=0
                )
                total = total + pick(rows, place_ref[2 * side + half])
        for p in range(CHUNK // 2):
            lanes = pl.ds(pl.multiple_of(chunk * (CHUNK * LEAF) + p * LANES, LANES), LANES)
            near_out[:, lanes] = total[p * RHS : (p + 1) * RHS]
        return carry

    chunks = leaves // CHUNK
    lax.fori_loop(0, chunks // 2, near_chunk, 0)

    lax.fori_loop(1, nleaf, wait_leaf, 0)

    def add(i, total):
        return total + gathered_ref[i, 8:16]

    total = lax.fori_loop(0, nleaf, add, jnp.zeros((8, KR), f32))
    sums[...] = total
    group_ref[g] = total
    for d in range(1, ngroup):
        group_copy(d, True).start()

    lax.fori_loop(chunks // 2, chunks, near_chunk, 0)

    finish(moves[1])
    for part in range(-(-3 * leaves // LANES)):
        turn(coef_ext, part * LANES, ct, part * LANES)
    local = (leaf_source_ref[...] - (device - 1) * leaves).astype(f32)
    lane = iota((leaves, slots), 1)
    expanded = mm(local.astype(bf16), mask(lane // FAR0 == iota((leaves, slots), 0)))
    lane = iota((FAR0, slots), 1)
    wanted = jnp.sum(jnp.where(lane % FAR0 == iota((FAR0, slots), 0), expanded, 0.0), axis=0, keepdims=True)
    onehot = mask(iota((ct.shape[1], slots), 0) == wanted.astype(jnp.int32))
    gl[...] = pick(ct[...], onehot)
    small_products(lt, gl, lwork, slots // LANES)

    for d in range(1, ngroup):
        group_copy(d, False).wait()
    count = gt.shape[1]
    rows = nleaf * 16
    for part in range(-(-rows // LANES)):
        first = part * LANES // 16
        here = min(LANES // 16, nleaf - first)
        turn(gathered_ref[first : first + here].reshape(here * 16, KR), 0, gt, part * LANES)
    turn(group_ref[...].reshape(ngroup * 8, KR), 0, gt, count - LANES)
    sources = cluster_source_ref[...]
    lane = iota((1, LANES), 1)
    wanted = jnp.full((1, LANES), -1, jnp.int32)
    for u in range(cpd):
        for j in range(FAR1):
            wanted = jnp.where(lane == u * FAR1 + j, sources[u : u + 1, j : j + 1], wanted)
    wanted = jnp.where(wanted >= 0, wanted // cpd * 16 + wanted % cpd, -1)
    wanted = jnp.where((lane >= wide) & (lane < wide + ngroup), count - LANES + 8 * (lane - wide), wanted)
    onehot = mask(iota((count, LANES), 0) == wanted)
    small_g[...] = pick(gt[...], onehot)
    small_products(st, small_g, work, 1)
    a, b = t, q
    mine = (b >= base) & (b < base + cpd)
    top = mask((a >= wide) & (a < wide + ngroup) & mine)
    small_g[...] = pick(work[...], top)
    slot = mask((a < wide) & (b - base == a // FAR1))
    far = pick(work[...], slot)
    small_products(st, small_g, work, 1, transposed=True)
    spread = mask((a - base == b // per) & (b < leaves))
    small_g[...] = pick(far + work[...], spread)
    small_products(et, small_g, work, 1, transposed=True)
    gather = mask(iota((slots, LANES), 0) // FAR0 == iota((slots, LANES), 1))
    field = work[...] + pick(lwork[...], gather)
    for c in range(K // 2):
        field_ref[:, c, :] = field[c * 2 * RHS : (c + 1) * 2 * RHS].T[:leaves]


def sum_kernel(near_ref, basis_ref, field_ref, out_ref):
    first = iota((RHS, LANES), 1) < LEAF

    def step(p, carry):
        ends = []
        for side in range(2):
            i = 2 * p + side
            fh, fl = halves(field_ref[i])
            bh, bl = halves(basis_ref[i])
            wide = mm(jnp.concatenate([fh, fl], axis=1), jnp.concatenate([bh, bl], axis=1), TN)
            both = wide[: 2 * RHS, :LANES] + wide[: 2 * RHS, LANES:] + wide[2 * RHS :, :LANES]
            ends.append((both[:RHS], both[RHS:]))
        straight = jnp.where(first, ends[0][0], ends[1][1])
        crossed = jnp.where(first, ends[1][0], ends[0][1])
        lanes = pl.ds(pl.multiple_of(p * LANES, LANES), LANES)
        out_ref[:, lanes] = near_ref[:, lanes] + straight + pltpu.roll(crossed, LEAF, 1)
        return carry

    lax.fori_loop(0, basis_ref.shape[0] // 2, step, 0, unroll=8)


def params(mib=48, **kw):
    return pltpu.CompilerParams(vmem_limit_bytes=mib * 1024 * 1024, **kw)


def per_device(
    right_sides,
    near_blocks,
    near_source,
    near_count,
    basis,
    leaf_source,
    leaf_coupling,
    leaf_transfer,
    cluster_source,
    cluster_coupling,
    cluster_transfer,
    group_coupling,
):
    leaves = near_blocks.shape[0]
    cpd = cluster_coupling.shape[0]
    ngroup, nleaf = lax.axis_size("group"), lax.axis_size("leaf")
    wide = cpd * FAR1
    base = wide + 8
    assert ngroup <= 8 and cpd <= 8 and base + 8 <= LANES and leaves <= LANES
    rows = nleaf * 16
    padded = -(-rows // LANES) * LANES
    source_lanes = -(-3 * leaves // LANES) * LANES
    slots = leaves * FAR0
    near, field, basis3 = pl.pallas_call(
        functools.partial(tree_kernel, base, cpd, nleaf, ngroup),
        out_shape=(
            jax.ShapeDtypeStruct((RHS, leaves * LEAF), f32),
            jax.ShapeDtypeStruct((leaves, K // 2, 2 * RHS), f32),
            jax.ShapeDtypeStruct((leaves, K * LEAF // LANES, LANES), f32),
        ),
        in_specs=[SMEM] * 2 + [VMEM] * 6 + [pl.BlockSpec(memory_space=pl.ANY)] * 4,
        out_specs=(VMEM, VMEM, VMEM),
        scratch_shapes=[
            pltpu.VMEM((leaves, K // 2, 2 * RHS), f32),
            pltpu.VMEM((leaves, KR), f32),
            pltpu.VMEM((RHS, leaves * LEAF), f32),
            pltpu.VMEM((leaves, KK), f32),
            pltpu.VMEM((base + 8, KK), f32),
            pltpu.VMEM((leaves, NEAR, LEAF * LEAF), f32),
            pltpu.VMEM((slots, KK), f32),
            pltpu.VMEM((RHS, leaves * LEAF), f32),
            pltpu.VMEM((RHS, leaves * LEAF), f32),
            pltpu.VMEM((3 * leaves, KR), f32),
            pltpu.VMEM((16, KR), f32),
            pltpu.VMEM((nleaf, 16, KR), f32),
            pltpu.VMEM((ngroup, 8, KR), f32),
            pltpu.VMEM((8, KR), f32),
            pltpu.VMEM((3 * leaves + 1, 2 * RHS, LANES), bf16),
            pltpu.VMEM((3 * leaves + 1, 2 * RHS, LANES), bf16),
            pltpu.VMEM((4, 2 * LANES, LANES), bf16),
            pltpu.VMEM((CHUNK, 2 * RHS, 2 * LANES), f32),
            pltpu.VMEM((KK, LANES), f32),
            pltpu.VMEM((KR, source_lanes), f32),
            pltpu.VMEM((KK, LANES), f32),
            pltpu.VMEM((KK, slots), f32),
            pltpu.VMEM((KR, padded + LANES), f32),
            pltpu.VMEM((KR, slots), f32),
            pltpu.VMEM((KR, LANES), f32),
            pltpu.VMEM((KR, slots), f32),
            pltpu.VMEM((KR, LANES), f32),
            pltpu.SemaphoreType.DMA((4,)),
            pltpu.SemaphoreType.DMA((4,)),
            pltpu.SemaphoreType.DMA((4,)),
            pltpu.SemaphoreType.DMA((nleaf,)),
            pltpu.SemaphoreType.DMA((nleaf,)),
            pltpu.SemaphoreType.DMA((ngroup,)),
            pltpu.SemaphoreType.DMA((ngroup,)),
        ],
        compiler_params=params(63, collective_id=0, has_side_effects=True),
        name="tree_and_near",
    )(
        near_source.T,
        near_count,
        basis,
        leaf_source.T,
        cluster_source,
        cluster_coupling.reshape(wide, KK),
        group_coupling.reshape(ngroup, KK),
        cluster_transfer,
        right_sides,
        leaf_transfer,
        near_blocks,
        leaf_coupling.reshape(slots, KK),
    )
    return pl.pallas_call(
        sum_kernel,
        out_shape=jax.ShapeDtypeStruct((RHS, leaves * LEAF), f32),
        in_specs=[VMEM] * 3,
        out_specs=VMEM,
        compiler_params=params(),
        name="sum",
    )(near, basis3, field)


def solution(mesh):
    split = P(("group", "leaf"))
    in_specs = (
        P(None, ("group", "leaf")),
        split,
        split,
        split,
        split,
        split,
        split,
        split,
        split,
        split,
        split,
        P("group"),
    )
    return jax.shard_map(
        per_device, mesh=mesh, in_specs=in_specs, out_specs=P(None, ("group", "leaf")), check_vma=False
    )
```

```python
import functools

import jax
import jax.numpy as jnp
from jax import lax
from jax.experimental import pallas as pl
from jax.experimental.pallas import tpu as pltpu
from jax.sharding import PartitionSpec as P

LEAF = 64
K = 32
RHS = 16
FAR0 = 8
FAR1 = 8
NEAR = 8
LANES = 128
KR = K * RHS
KK = K * K
CHUNK = 8

f32 = jnp.float32
bf16 = jnp.bfloat16
MESH = pl.DeviceIdType.MESH
VMEM = pl.BlockSpec(memory_space=pltpu.VMEM)
SMEM = pl.BlockSpec(memory_space=pltpu.SMEM)
NT = (((1,), (1,)), ((), ()))
NN = (((1,), (0,)), ((), ()))
TN = (((0,), (0,)), ((), ()))


def halves(value):
    high = value.astype(bf16)
    low = (value - high.astype(f32)).astype(bf16)
    return high, low


def mm(a, b, dims=NN):
    return lax.dot_general(a, b, dims, preferred_element_type=f32)


def pick(value, chosen):
    high, low = halves(value)
    return mm(high, chosen) + mm(low, chosen)


def iota(shape, dim):
    return lax.broadcasted_iota(jnp.int32, shape, dim)


def mask(condition):
    return jnp.where(condition, 1.0, 0.0).astype(bf16)


def doubled_pair(pair):
    first = iota(pair.shape, 1) < LEAF
    turned = pltpu.roll(pair, LEAF, 1)
    zero = jnp.zeros_like(pair)
    even = jnp.concatenate([jnp.where(first, pair, zero), jnp.where(first, zero, turned)], axis=0)
    odd = jnp.concatenate([jnp.where(first, turned, zero), jnp.where(first, zero, pair)], axis=0)
    return even, odd


def coef_kernel(x_ref, basis_ref, coef_ref):
    def step(p, carry):
        pair = x_ref[:, pl.ds(pl.multiple_of(p * LANES, LANES), LANES)]
        for side, doubled in enumerate(doubled_pair(pair)):
            xh, xl = halves(doubled)
            bh, bl = halves(basis_ref[2 * p + side])
            both = jnp.concatenate([bh, bl], axis=1)
            twice = jnp.concatenate([xh, xh], axis=1)
            coef_ref[2 * p + side] = mm(both, twice, NT) + mm(bh, xl, NT)
        return carry

    lax.fori_loop(0, basis_ref.shape[0] // 2, step, 0, unroll=8)


def turn(src, rows, dst_ref, lane):
    here = min(LANES, src.shape[0] - rows)
    for c in range(src.shape[1] // LANES):
        block = src[rows : rows + here, c * LANES : (c + 1) * LANES]
        if here < LANES:
            block = jnp.concatenate([block, jnp.zeros((LANES - here, LANES), f32)], axis=0)
        dst_ref[c * LANES : (c + 1) * LANES, lane : lane + LANES] = block.T


def small_products(at_ref, g_ref, out_ref, tiles, transposed=False):
    width = 8

    def step(i, carry):
        tile, kb = i // (K // width), i % (K // width)
        lanes = pl.ds(pl.multiple_of(tile * LANES, LANES), LANES)
        acc = [jnp.zeros((RHS, LANES), f32)] * width
        for l8 in range(0, K, 8):
            if transposed:
                at = [at_ref[pl.ds(pl.multiple_of(kb * 8, 8) + l * K, 8), lanes] for l in range(l8, l8 + 8)]
            else:
                at = [at_ref[pl.ds(pl.multiple_of(kb * 8 * K, 8 * K) + j * K + l8, 8), lanes] for j in range(width)]
            for i in range(8):
                g = g_ref[(l8 + i) * RHS : (l8 + i + 1) * RHS, lanes]
                for j in range(width):
                    row = at[i][j : j + 1] if transposed else at[j][i : i + 1]
                    acc[j] = acc[j] + row * g
        for j in range(width):
            start = pl.multiple_of(kb * (width * RHS) + j * RHS, RHS)
            out_ref[pl.ds(start, RHS), lanes] = acc[j]
        return carry

    lax.fori_loop(0, tiles * (K // width), step, 0)


def tree_kernel(base, cpd, nleaf, ngroup,
                source_ref, count_ref, basis_in_ref, leaf_source_ref, cluster_source_ref,
                cluster_coupling_ref, group_coupling_ref, cluster_transfer_ref,
                x_hbm, transfer_hbm, near_hbm, coupling_hbm,
                out_ref,
                near_out, field_ref, basis_ref, coef_blocks, coef_ref, x_ref, transfer_ref, small_ref, near_ref, coupling_ref, xb, xa, coef_ext, block_ref, gathered_ref, group_ref, sums,
                xh_ref, xl_ref, place_ref, part_ref,
                et, ct, st, lt, gt, gl, work, lwork, small_g,
                local_sem, x_sem, coef_sem, leaf_send, leaf_recv, group_send, group_recv):
    leaves = transfer_ref.shape[0]
    per = leaves // cpd
    slots = leaves * FAR0
    wide = cpd * FAR1
    g, z = lax.axis_index("group"), lax.axis_index("leaf")
    size = nleaf * ngroup
    device = g * nleaf + z
    following, preceding = lax.rem(device + 1, size), lax.rem(device + size - 1, size)
    next_id = (following // nleaf, lax.rem(following, nleaf))
    prev_id = (preceding // nleaf, lax.rem(preceding, nleaf))
    has_next, has_prev = device < size - 1, device > 0
    cross_next = has_next & (z == nleaf - 1)
    cross_prev = has_prev & (z == 0)

    near_copy = pltpu.make_async_copy(near_hbm, near_ref, local_sem.at[0])
    coupling_copy = pltpu.make_async_copy(coupling_hbm, coupling_ref, local_sem.at[1])
    x_copy = pltpu.make_async_copy(x_hbm, x_ref, local_sem.at[2])
    transfer_copy = pltpu.make_async_copy(transfer_hbm, transfer_ref, local_sem.at[3])
    x_copy.start()
    transfer_copy.start()
    coupling_copy.start()
    near_copy.start()

    barrier = pltpu.get_barrier_semaphore()

    def greet_leaf(d, carry):
        pl.semaphore_signal(barrier, inc=1, device_id=(g, lax.rem(z + d, nleaf)), device_id_type=MESH)
        return carry

    def greet_group(d, carry):
        pl.semaphore_signal(barrier, inc=1, device_id=(lax.rem(g + d, ngroup), z), device_id_type=MESH)
        return carry

    lax.fori_loop(1, nleaf, greet_leaf, 0)
    lax.fori_loop(1, ngroup, greet_group, 0)

    @pl.when(cross_next)
    def _():
        pl.semaphore_signal(barrier, inc=1, device_id=next_id, device_id_type=MESH)

    @pl.when(cross_prev)
    def _():
        pl.semaphore_signal(barrier, inc=1, device_id=prev_id, device_id_type=MESH)

    def build(ref, part):
        def step(p, carry):
            pair = ref[:, pl.ds(pl.multiple_of(p * LANES, LANES), LANES)]
            for side, doubled in enumerate(doubled_pair(pair)):
                high, low = halves(doubled)
                xh_ref[part * leaves + 2 * p + side] = high
                xl_ref[part * leaves + 2 * p + side] = low
            return carry

        lax.fori_loop(0, leaves // 2, step, 0, unroll=8)


    @pl.when(jnp.logical_not(has_prev))
    def _():
        xb[...] = jnp.zeros_like(xb)
        coef_ext[0:leaves] = jnp.zeros((leaves, KR), f32)

    @pl.when(jnp.logical_not(has_next))
    def _():
        xa[...] = jnp.zeros_like(xa)
        coef_ext[2 * leaves : 3 * leaves] = jnp.zeros((leaves, KR), f32)

    enough = nleaf + ngroup - 2
    crossing = cross_next | cross_prev

    @pl.when(crossing)
    def _():
        pl.semaphore_wait(barrier, enough + 1)

    @pl.when(jnp.logical_not(crossing))
    def _():
        pl.semaphore_wait(barrier, enough)

    def to_next(src, dst, sem):
        return pltpu.make_async_remote_copy(
            src_ref=src, dst_ref=dst, send_sem=sem.at[0], recv_sem=sem.at[2], device_id=next_id, device_id_type=MESH)

    def to_prev(src, dst, sem):
        return pltpu.make_async_remote_copy(
            src_ref=src, dst_ref=dst, send_sem=sem.at[1], recv_sem=sem.at[3], device_id=prev_id, device_id_type=MESH)

    moves = (
        (x_hbm, xb, xa, x_sem),
        (coef_ref, coef_ext.at[pl.ds(0, leaves)], coef_ext.at[pl.ds(2 * leaves, leaves)], coef_sem),
    )

    def send(move):
        src, before, after, sem = move

        @pl.when(has_next)
        def _():
            to_next(src, before, sem).start()

        @pl.when(has_prev)
        def _():
            to_prev(src, after, sem).start()

    send(moves[0])

    def finish(move):
        src, before, after, sem = move

        @pl.when(has_next)
        def _():
            to_next(src, before, sem).wait_send()
            to_prev(src, after, sem).wait_recv()

        @pl.when(has_prev)
        def _():
            to_prev(src, after, sem).wait_send()
            to_next(src, before, sem).wait_recv()

    for c in range(K * LEAF // LANES):
        basis_ref[:, c, :] = basis_in_ref[:, c * LANES : (c + 1) * LANES]
    x_copy.wait()
    coef_kernel(x_ref, basis_ref, coef_blocks)
    ct[...] = jnp.zeros_like(ct)
    for c in range(K // 2):
        ct[c * 2 * RHS : (c + 1) * 2 * RHS, 0:leaves] = coef_blocks[:, c, :].T
    for c in range(KR // LANES):
        rows = slice(c * LANES, (c + 1) * LANES)
        coef_ref[:, rows] = ct[rows, 0:LANES].T[:leaves]
    coef_ext[leaves : 2 * leaves] = coef_ref[...]
    send(moves[1])

    small_ref[...] = jnp.zeros_like(small_ref)
    small_ref[0:wide] = cluster_coupling_ref[...]
    small_ref[wide : wide + ngroup] = group_coupling_ref[...]
    small_ref[base : base + cpd] = cluster_transfer_ref[...]
    turn(small_ref, 0, st, 0)
    transfer_copy.wait()
    turn(transfer_ref, 0, et, 0)
    small_products(et, ct, work, 1)
    t, q = iota((LANES, LANES), 0), iota((LANES, LANES), 1)
    chosen = mask((q - base == t // per) & (t < leaves))
    small_g[...] = pick(work[...], chosen)
    small_products(st, small_g, work, 1)
    for c in range(KR // LANES):
        rows = slice(c * LANES, (c + 1) * LANES)
        block_ref[0:8, rows] = small_g[rows, :].T[base : base + 8]
        total = jnp.sum(work[rows, :].T[base : base + cpd], axis=0, keepdims=True)
        block_ref[8:16, rows] = jnp.broadcast_to(total, (8, LANES))

    def to_leaf(d):
        return pltpu.make_async_remote_copy(
            src_ref=block_ref, dst_ref=gathered_ref.at[z], send_sem=leaf_send.at[d], recv_sem=leaf_recv.at[z],
            device_id=(g, lax.rem(z + d, nleaf)), device_id_type=MESH)

    def from_leaf(d):
        peer = lax.rem(z + d, nleaf)
        return pltpu.make_async_remote_copy(
            src_ref=block_ref, dst_ref=gathered_ref.at[peer], send_sem=leaf_send.at[d], recv_sem=leaf_recv.at[peer],
            device_id=(g, peer), device_id_type=MESH)

    def start_leaf(d, carry):
        to_leaf(d).start()
        return carry

    def wait_leaf(d, carry):
        from_leaf(d).wait()
        return carry

    def group_copy(d, outgoing):
        peer = lax.rem(g + d, ngroup)
        at = g if outgoing else peer
        return pltpu.make_async_remote_copy(
            src_ref=sums, dst_ref=group_ref.at[at], send_sem=group_send.at[d], recv_sem=group_recv.at[at],
            device_id=(peer, z), device_id_type=MESH)

    lax.fori_loop(1, nleaf, start_leaf, 0)
    gathered_ref[z] = block_ref[...]

    build(x_ref, 1)
    xh_ref[3 * leaves] = jnp.zeros(xh_ref.shape[1:], bf16)
    xl_ref[3 * leaves] = jnp.zeros(xl_ref.shape[1:], bf16)
    row, col = iota((2 * LANES, LANES), 0), iota((2 * LANES, LANES), 1)
    for side in range(2):
        for half in range(2):
            place_ref[2 * side + half] = mask(col == side * LEAF + 2 * (row // NEAR) + half)
    coupling_copy.wait()
    for tile in range(slots // LANES):
        turn(coupling_ref, tile * LANES, lt, tile * LANES)
    finish(moves[0])
    build(xb, 0)
    build(xa, 2)
    near_copy.wait()

    slot_of_lane = iota((2 * RHS, 2 * LANES), 1) % NEAR

    def near_chunk(chunk, carry):
        for i in range(CHUNK):
            n = near_ref[chunk * CHUNK + i]
            rows = jnp.concatenate([n[:, c * LANES : (c + 1) * LANES] for c in range(LEAF // 2)], axis=0)
            nh, nl = halves(rows)
            weights = jnp.concatenate([nh, nl], axis=1)
            leaf = chunk * CHUNK + i
            live = count_ref[leaf]
            at = [
                jnp.where(j < live, source_ref[j, leaf] - (device - 1) * leaves, 3 * leaves) for j in range(NEAR)
            ]
            xh = jnp.concatenate([xh_ref[s] for s in at], axis=0)
            xl = jnp.concatenate([xl_ref[s] for s in at], axis=0)
            full = mm(jnp.concatenate([xh, xh], axis=1), weights, NT) + mm(
                jnp.concatenate([xl, xl], axis=1), weights, NT
            )
            kept = full[: 2 * RHS]
            for j in range(1, NEAR):
                kept = jnp.where(slot_of_lane == j, full[j * 2 * RHS : (j + 1) * 2 * RHS], kept)
            part_ref[i] = kept
        total = jnp.zeros((CHUNK // 2 * RHS, LANES), f32)
        for side in range(2):
            for half in range(2):
                rows = jnp.concatenate(
                    [part_ref[2 * p + side, half * RHS : (half + 1) * RHS] for p in range(CHUNK // 2)], axis=0
                )
                total = total + pick(rows, place_ref[2 * side + half])
        for p in range(CHUNK // 2):
            lanes = pl.ds(pl.multiple_of(chunk * (CHUNK * LEAF) + p * LANES, LANES), LANES)
            near_out[:, lanes] = total[p * RHS : (p + 1) * RHS]
        return carry

    chunks = leaves // CHUNK
    lax.fori_loop(0, chunks // 2, near_chunk, 0)

    lax.fori_loop(1, nleaf, wait_leaf, 0)

    def add(i, total):
        return total + gathered_ref[i, 8:16]

    total = lax.fori_loop(0, nleaf, add, jnp.zeros((8, KR), f32))
    sums[...] = total
    group_ref[g] = total
    for d in range(1, ngroup):
        group_copy(d, True).start()

    lax.fori_loop(chunks // 2, chunks, near_chunk, 0)

    finish(moves[1])
    for part in range(-(-3 * leaves // LANES)):
        turn(coef_ext, part * LANES, ct, part * LANES)
    local = (leaf_source_ref[...] - (device - 1) * leaves).astype(f32)
    lane = iota((leaves, slots), 1)
    expanded = mm(local.astype(bf16), mask(lane // FAR0 == iota((leaves, slots), 0)))
    lane = iota((FAR0, slots), 1)
    wanted = jnp.sum(jnp.where(lane % FAR0 == iota((FAR0, slots), 0), expanded, 0.0), axis=0, keepdims=True)
    onehot = mask(iota((ct.shape[1], slots), 0) == wanted.astype(jnp.int32))
    gl[...] = pick(ct[...], onehot)
    small_products(lt, gl, lwork, slots // LANES)

    for d in range(1, ngroup):
        group_copy(d, False).wait()
    count = gt.shape[1]
    rows = nleaf * 16
    for part in range(-(-rows // LANES)):
        first = part * LANES // 16
        here = min(LANES // 16, nleaf - first)
        turn(gathered_ref[first : first + here].reshape(here * 16, KR), 0, gt, part * LANES)
    turn(group_ref[...].reshape(ngroup * 8, KR), 0, gt, count - LANES)
    sources = cluster_source_ref[...]
    lane = iota((1, LANES), 1)
    wanted = jnp.full((1, LANES), -1, jnp.int32)
    for u in range(cpd):
        for j in range(FAR1):
            wanted = jnp.where(lane == u * FAR1 + j, sources[u : u + 1, j : j + 1], wanted)
    wanted = jnp.where(wanted >= 0, wanted // cpd * 16 + wanted % cpd, -1)
    wanted = jnp.where((lane >= wide) & (lane < wide + ngroup), count - LANES + 8 * (lane - wide), wanted)
    onehot = mask(iota((count, LANES), 0) == wanted)
    small_g[...] = pick(gt[...], onehot)
    small_products(st, small_g, work, 1)
    a, b = t, q
    mine = (b >= base) & (b < base + cpd)
    top = mask((a >= wide) & (a < wide + ngroup) & mine)
    small_g[...] = pick(work[...], top)
    slot = mask((a < wide) & (b - base == a // FAR1))
    far = pick(work[...], slot)
    small_products(st, small_g, work, 1, transposed=True)
    spread = mask((a - base == b // per) & (b < leaves))
    small_g[...] = pick(far + work[...], spread)
    small_products(et, small_g, work, 1, transposed=True)
    gather = mask(iota((slots, LANES), 0) // FAR0 == iota((slots, LANES), 1))
    field = work[...] + pick(lwork[...], gather)
    for c in range(K // 2):
        field_ref[:, c, :] = field[c * 2 * RHS : (c + 1) * 2 * RHS].T[:leaves]
    sum_kernel(near_out, basis_ref, field_ref, out_ref)


def sum_kernel(near_ref, basis_ref, field_ref, out_ref):
    first = iota((RHS, LANES), 1) < LEAF

    def step(p, carry):
        ends = []
        for side in range(2):
            i = 2 * p + side
            fh, fl = halves(field_ref[i])
            bh, bl = halves(basis_ref[i])
            wide = mm(jnp.concatenate([fh, fl], axis=1), jnp.concatenate([bh, bl], axis=1), TN)
            both = wide[: 2 * RHS, :LANES] + wide[: 2 * RHS, LANES:] + wide[2 * RHS :, :LANES]
            ends.append((both[:RHS], both[RHS:]))
        straight = jnp.where(first, ends[0][0], ends[1][1])
        crossed = jnp.where(first, ends[1][0], ends[0][1])
        lanes = pl.ds(pl.multiple_of(p * LANES, LANES), LANES)
        out_ref[:, lanes] = near_ref[:, lanes] + straight + pltpu.roll(crossed, LEAF, 1)
        return carry

    lax.fori_loop(0, basis_ref.shape[0] // 2, step, 0, unroll=8)


def params(mib=48, **kw):
    return pltpu.CompilerParams(vmem_limit_bytes=mib * 1024 * 1024, **kw)


def per_device(
    right_sides,
    near_blocks,
    near_source,
    near_count,
    basis,
    leaf_source,
    leaf_coupling,
    leaf_transfer,
    cluster_source,
    cluster_coupling,
    cluster_transfer,
    group_coupling,
):
    leaves = near_blocks.shape[0]
    cpd = cluster_coupling.shape[0]
    ngroup, nleaf = lax.axis_size("group"), lax.axis_size("leaf")
    wide = cpd * FAR1
    base = wide + 8
    assert ngroup <= 8 and cpd <= 8 and base + 8 <= LANES and leaves <= LANES
    rows = nleaf * 16
    padded = -(-rows // LANES) * LANES
    source_lanes = -(-3 * leaves // LANES) * LANES
    slots = leaves * FAR0
    return pl.pallas_call(
        functools.partial(tree_kernel, base, cpd, nleaf, ngroup),
        out_shape=jax.ShapeDtypeStruct((RHS, leaves * LEAF), f32),
        in_specs=[SMEM] * 2 + [VMEM] * 6 + [pl.BlockSpec(memory_space=pl.ANY)] * 4,
        out_specs=VMEM,
        scratch_shapes=[
            pltpu.VMEM((RHS, leaves * LEAF), f32),
            pltpu.VMEM((leaves, K // 2, 2 * RHS), f32),
            pltpu.VMEM((leaves, K * LEAF // LANES, LANES), f32),
            pltpu.VMEM((leaves, K // 2, 2 * RHS), f32),
            pltpu.VMEM((leaves, KR), f32),
            pltpu.VMEM((RHS, leaves * LEAF), f32),
            pltpu.VMEM((leaves, KK), f32),
            pltpu.VMEM((base + 8, KK), f32),
            pltpu.VMEM((leaves, NEAR, LEAF * LEAF), f32),
            pltpu.VMEM((slots, KK), f32),
            pltpu.VMEM((RHS, leaves * LEAF), f32),
            pltpu.VMEM((RHS, leaves * LEAF), f32),
            pltpu.VMEM((3 * leaves, KR), f32),
            pltpu.VMEM((16, KR), f32),
            pltpu.VMEM((nleaf, 16, KR), f32),
            pltpu.VMEM((ngroup, 8, KR), f32),
            pltpu.VMEM((8, KR), f32),
            pltpu.VMEM((3 * leaves + 1, 2 * RHS, LANES), bf16),
            pltpu.VMEM((3 * leaves + 1, 2 * RHS, LANES), bf16),
            pltpu.VMEM((4, 2 * LANES, LANES), bf16),
            pltpu.VMEM((CHUNK, 2 * RHS, 2 * LANES), f32),
            pltpu.VMEM((KK, LANES), f32),
            pltpu.VMEM((KR, source_lanes), f32),
            pltpu.VMEM((KK, LANES), f32),
            pltpu.VMEM((KK, slots), f32),
            pltpu.VMEM((KR, padded + LANES), f32),
            pltpu.VMEM((KR, slots), f32),
            pltpu.VMEM((KR, LANES), f32),
            pltpu.VMEM((KR, slots), f32),
            pltpu.VMEM((KR, LANES), f32),
            pltpu.SemaphoreType.DMA((4,)),
            pltpu.SemaphoreType.DMA((4,)),
            pltpu.SemaphoreType.DMA((4,)),
            pltpu.SemaphoreType.DMA((nleaf,)),
            pltpu.SemaphoreType.DMA((nleaf,)),
            pltpu.SemaphoreType.DMA((ngroup,)),
            pltpu.SemaphoreType.DMA((ngroup,)),
        ],
        compiler_params=params(63, collective_id=0, has_side_effects=True),
        name="tree_and_near",
    )(
        near_source.T,
        near_count,
        basis,
        leaf_source.T,
        cluster_source,
        cluster_coupling.reshape(wide, KK),
        group_coupling.reshape(ngroup, KK),
        cluster_transfer,
        right_sides,
        leaf_transfer,
        near_blocks,
        leaf_coupling.reshape(slots, KK),
    )


def solution(mesh):
    split = P(("group", "leaf"))
    in_specs = (
        P(None, ("group", "leaf")),
        split,
        split,
        split,
        split,
        split,
        split,
        split,
        split,
        split,
        split,
        P("group"),
    )
    return jax.shard_map(
        per_device, mesh=mesh, in_specs=in_specs, out_specs=P(None, ("group", "leaf")), check_vma=False
    )
```
